512 devices in a mesh: space: 128 (over z, x, core), basis: 4 (over y).
Axes of the slice: x: 4, y: 4, z: 16, core: 2. Of those that a mesh axis runs over, the one named last changes fastest.
Arguments:
- x_block: float32 [16, 3, 128, 32, 128], P(None, None, 'space', 'basis'), may hold values from -68 to 68
- basis: float32 [64, 3, 128, 32, 128], P('basis', None, 'space'), may hold values from -11 to 11
- material: int32 [128, 32, 128], P('space', 'basis'), may hold values from 0 to 7
- k0_blocks: float32 [8, 7, 3, 3], replicated, may hold values from -4 to 4
- k0_diag: float32 [8, 3], replicated, may hold values from 2 to 8
- ke_blocks: float32 [8, 7, 3, 3], replicated, may hold values from -6 to 6
- mass: float32 [8, 3], replicated, may hold values from 0.5 to 2
- velocities: float32 [1024], replicated, may hold values from 0.5 to 1
- shifts: float32 [1024], replicated, may hold values from 0.5 to 1.5
- sample: int32 [1], replicated, may hold values from 0 to 1023
Outputs:
- orthonormal: float32 [16, 3, 128, 32, 128], P(None, None, 'space', 'basis')
- coefficients: float32 [64, 16], P('basis')
- upper_factor: float32 [16, 16], replicated
The draws below stay inside these ranges and needn't reach their ends.
All inputs are finite; a program needn't handle non-finite values.
Results may differ from the reference program's by a relative error of at most 0.00015.
Values sent between devices are 32-bit elements; how exact they have to be, the bound alone decides.
A program may use at most 64 MiB of HBM per device.

```python
import math
import jax
import jax.numpy as jnp
from jax import lax

BLOCK = 16
BASIS_COLS = 64
NMAT = 8
NSAMP = 1024
GX = 128
GY = 32
GZ = 128


def shared_fields(key):
    keys = [jax.random.fold_in(key, 100 + index) for index in range(8)]
    cell_shape = (GX, GY, GZ)
    basis_shape = (BASIS_COLS, 3, GX, GY, GZ)
    noise = jnp.clip(jax.random.normal(keys[0], basis_shape, jnp.float32), -4.0, 4.0)
    weight = 0.15
    common = jnp.clip(jax.random.normal(keys[1], (3, GX, GY, GZ), jnp.float32), -4.0, 4.0)
    signs = 2.0 * jax.random.randint(keys[2], (BASIS_COLS,), 0, 2).astype(jnp.float32) - 1.0
    spread = jax.random.uniform(keys[3], cell_shape, jnp.float32)
    position = (jnp.arange(GX).astype(jnp.float32) / GX)[:, None, None]
    row_scale = jnp.exp(jnp.log(10.0) * (0.5 * position + 0.5 * spread))
    basis = 0.22 * row_scale * (noise + weight * signs[:, None, None, None, None] * common)
    return (basis, keys, row_scale)


def draw_basis(key, part):
    return shared_fields(key)[0]


def draw_x_block(key, part):
    basis, keys, row_scale = shared_fields(key)
    groups = BASIS_COLS // BLOCK
    mix_signs = 2.0 * jax.random.randint(keys[4], (groups, 4, BLOCK), 0, 2).astype(jnp.float32) - 1.0
    mixing = jax.random.uniform(keys[5], (groups, 4, BLOCK), jnp.float32, 0.5, 1.5) * mix_signs
    extra = jnp.clip(jax.random.normal(keys[6], (BLOCK, 3, GX, GY, GZ), jnp.float32), -4.0, 4.0)
    result = 0.11 * row_scale * extra
    columns = jnp.arange(BLOCK)
    for group in range(groups):
        for band in range(4):
            chosen = group * BLOCK + (columns + band) % BLOCK
            result = result + 0.25 * mixing[group, band][:, None, None, None, None] * basis[chosen]
    return result


def place_ends(values, own_key, least, high):
    spot = [jax.random.randint(jax.random.fold_in(own_key, axis), (), 0, length) for axis, length in enumerate(values.shape)]
    main_axis = values.shape.index(max(values.shape))
    beside = spot[:main_axis] + [(spot[main_axis] + 1) % values.shape[main_axis]] + spot[main_axis + 1:]
    return values.at[tuple(spot)].set(least).at[tuple(beside)].set(high)


def normal_values(key, extent, scale, bound, kind=jnp.bfloat16):
    drawn = scale * jax.random.normal(key, extent, jnp.float32)
    return jnp.clip(drawn, min=-bound, max=bound).astype(kind)


def setup_inputs(seed: int = 0) -> dict:
    key_list = jax.random.split(jax.random.key(seed), 11)
    return {
        "x_block": draw_x_block(jax.random.fold_in(key_list[10], 71), 0),
        "basis": draw_basis(jax.random.fold_in(key_list[10], 71), 0),
        "material": place_ends(jax.random.randint(key_list[2], (GX, GY, GZ), 0, NMAT), jax.random.fold_in(key_list[2], 1), 0, NMAT - 1).astype(jnp.int32),
        "k0_blocks": normal_values(key_list[3], (NMAT, 7, 3, 3), 0.3, 4.0, jnp.float32),
        "k0_diag": jnp.clip(jnp.exp(jax.random.uniform(key_list[4], (NMAT, 3), jnp.float32, math.log(2.0), math.log(8.0))), 2.0, 8.0),
        "ke_blocks": normal_values(key_list[5], (NMAT, 7, 3, 3), 0.5, 6.0, jnp.float32),
        "mass": jnp.clip(jnp.exp(jax.random.uniform(key_list[6], (NMAT, 3), jnp.float32, math.log(0.5), math.log(2.0))), 0.5, 2.0),
        "velocities": jnp.clip(jax.random.uniform(key_list[7], (NSAMP,), jnp.float32, 0.5, 1.0), 0.5, 1.0),
        "shifts": jnp.clip(jax.random.uniform(key_list[8], (NSAMP,), jnp.float32, 0.5, 1.5), 0.5, 1.5),
        "sample": jax.random.randint(key_list[9], (1,), 0, NSAMP).astype(jnp.int32),
    }


exact_precision = lax.Precision.HIGHEST

def stencil_tables(k0_blocks, k0_diag, ke_blocks, mass, velocities, shifts, sample):
    velocity = jnp.take(velocities, sample, axis=0)[0]
    sigma_value = jnp.take(shifts, sample, axis=0)[0]
    center = (k0_diag - sigma_value * mass)[:, :, None] * jnp.eye(3, dtype=jnp.float32)
    tables = k0_blocks - velocity * velocity * ke_blocks
    return tables.at[:, 0].add(center)

def neighbour_views(padded):
    extent_x = padded.shape[2] - 2
    extent_y = padded.shape[3] - 2
    extent_z = padded.shape[4] - 2

    def window(step_x, step_y, step_z):
        return padded[:, :, 1 + step_x:1 + step_x + extent_x, 1 + step_y:1 + step_y + extent_y, 1 + step_z:1 + step_z + extent_z]
    return [window(0, 0, 0), window(-1, 0, 0), window(1, 0, 0), window(0, -1, 0), window(0, 1, 0), window(0, 0, -1), window(0, 0, 1)]

def reference(x_block, basis, material, k0_blocks, k0_diag, ke_blocks, mass, velocities, shifts, sample):
    tables = stencil_tables(k0_blocks, k0_diag, ke_blocks, mass, velocities, shifts, sample)
    cell_blocks = tables[material]
    padded = jnp.pad(x_block, ((0, 0), (0, 0), (1, 1), (1, 1), (1, 1)))
    stencil_views = neighbour_views(padded)
    applied = jnp.zeros(x_block.shape, jnp.float32)
    for offset in range(7):
        applied = applied + jnp.einsum('xyzij,njxyz->nixyz', cell_blocks[:, :, :, offset], stencil_views[offset], precision=exact_precision)
    row_count = 3.0 * GX * GY * GZ
    running = jnp.zeros((BASIS_COLS, BLOCK), jnp.float32)
    for repeat in range(2):
        coeffs = jnp.einsum('kcxyz,ncxyz->kn', basis, applied, precision=exact_precision) / row_count
        applied = applied - jnp.einsum('kcxyz,kn->ncxyz', basis, coeffs, precision=exact_precision)
        running = running + coeffs
    gram_matrix = jnp.einsum('ncxyz,mcxyz->nm', applied, applied, precision=exact_precision) / row_count
    lower_factor = jnp.linalg.cholesky(gram_matrix)
    inverse = jax.scipy.linalg.solve_triangular(lower_factor, jnp.eye(BLOCK, dtype=jnp.float32), lower=True).T
    orthonormal = jnp.einsum('mcxyz,mn->ncxyz', applied, inverse, precision=exact_precision)
    return (orthonormal, running, lower_factor.T)
```

```python
import functools

import jax
import jax.numpy as jnp
from jax import lax
from jax.experimental import pallas as pl
from jax.experimental.pallas import tpu as pltpu
from jax.sharding import PartitionSpec as P

MESH = pl.DeviceIdType.MESH
PLANE = 8
EXACT = lax.Precision.HIGHEST
F32 = jnp.float32
BF16 = jnp.bfloat16


def dot_exact(a, b):
    return lax.dot_general(
        a, b, (((1,), (0,)), ((), ())), precision=EXACT, preferred_element_type=F32
    )


def iota(shape, axis):
    return lax.broadcasted_iota(jnp.int32, shape, axis)


def pick(bits, values):
    level = list(values)
    for bit in bits:
        level = [jnp.where(bit, level[i + 1], level[i]) for i in range(0, len(level), 2)]
    return level[0]


def fill_fields(mat_ref, k0, ke, diag, mass, velocities, shifts, sample, fields):
    index = sample[0, 0]
    velocity = velocities[index // 128, index % 128]
    shift = shifts[index // 128, index % 128]
    square = velocity * velocity
    cells = mat_ref[0]
    bits = [((cells >> b) & 1) == 1 for b in range(3)]

    def offset_body(o, carry):
        for i in range(3):
            for j in range(3):
                values = [k0[i, j, m, o] - square * ke[i, j, m, o] for m in range(8)]
                fields[o * 9 + i * 3 + j] = pick(bits, values)
        return carry

    lax.fori_loop(0, 7, offset_body, 0)
    for i in range(3):
        values = [diag[i, m] - shift * mass[i, m] for m in range(8)]
        fields[4 * i] = fields[4 * i] + pick(bits, values)


def apply_stencil(xs, xh, yh, fields, applied):
    row = iota((8, 128), 0)
    lane = iota((8, 128), 1)

    def column(n, carry):
        sums = [None] * 3
        for j in range(3):
            centre = xs[n, j]
            low_y = jnp.where(
                row == 0, jnp.broadcast_to(yh[0, n, j], (8, 128)), pltpu.roll(centre, 1, 0)
            )
            high_y = jnp.where(
                row == 7, jnp.broadcast_to(yh[1, n, j], (8, 128)), pltpu.roll(centre, 7, 0)
            )
            low_z = jnp.where(lane == 0, 0.0, pltpu.roll(centre, 1, 1))
            high_z = jnp.where(lane == 127, 0.0, pltpu.roll(centre, 127, 1))
            views = [centre, xh[0, n, j], xh[1, n, j], low_y, high_y, low_z, high_z]
            for o in range(7):
                for i in range(3):
                    term = fields[o * 9 + i * 3 + j] * views[o]
                    sums[i] = term if sums[i] is None else sums[i] + term
        for i in range(3):
            applied[n, i] = sums[i]
        return carry

    lax.fori_loop(0, 16, column, 0)


def split_rows(raw, data, first):
    def tile(t, carry):
        block = raw[pl.ds(t, 16, stride=24), :]
        high = block.astype(BF16)
        rest = (block - high.astype(F32)).astype(BF16)
        lanes = pl.ds(pl.multiple_of(t * 128, 128), 128)
        data[pl.ds(first, 16), lanes] = high
        data[pl.ds(80 + first, 16), lanes] = rest
        return carry

    lax.fori_loop(0, 24, tile, 0, unroll=4)


def pack_upper(full, packed):
    lane = iota((16, 128), 1)
    rows = [full[16 * g : 16 * g + 16, :] for g in range(5)]
    packed[0:16, :] = jnp.where(lane < 80, rows[0], pltpu.roll(rows[2], 48, 1))
    packed[16:32, :] = jnp.where(
        lane < 64,
        pltpu.roll(rows[1], 112, 1),
        jnp.where(
            lane < 96,
            pltpu.roll(rows[3], 16, 1),
            jnp.where(lane < 112, pltpu.roll(rows[4], 32, 1), 0.0),
        ),
    )


def unpack_full(packed, scale):
    lane = iota((16, 128), 1)
    one, two = packed[0:16, :], packed[16:32, :]
    parts = [
        one,
        pltpu.roll(two, 16, 1),
        pltpu.roll(one, 80, 1),
        pltpu.roll(two, 112, 1),
        pltpu.roll(two, 96, 1),
    ]
    rows = []
    for g in range(5):
        weight = jnp.where(lane < 16 * g + 16, 0.5 * scale, scale)
        rows.append(jnp.where((lane >= 16 * g) & (lane < 80), parts[g] * weight, 0.0))
    rows.append(jnp.zeros((48, 128), F32))
    upper = jnp.concatenate(rows, axis=0)
    return upper + upper.T


def factor(gram):
    row = iota((16, 128), 0)
    lane = iota((16, 128), 1)
    work = jnp.where(lane < 16, gram, jnp.where(lane == row + 16, 1.0, 0.0))
    for k in range(15):
        pivot_row = jnp.broadcast_to(work[k : k + 1, :], (16, 128))
        column = jnp.broadcast_to(work[:, k : k + 1], (16, 128))
        pivot = jnp.broadcast_to(work[k : k + 1, k : k + 1], (16, 128))
        work = work - jnp.where(row > k, column / pivot, 0.0) * pivot_row
    pivots = jnp.sum(jnp.where(lane == row, work, 0.0), axis=1, keepdims=True)
    root = lax.rsqrt(pivots)
    root = root * (1.5 - 0.5 * pivots * root * root)
    return work * root


def kernel(
    sizes,
    x_hbm, basis_hbm, mat_hbm, k0_hbm, ke_hbm, diag_hbm, mass_hbm, vel_hbm, shift_hbm, sample_hbm,
    ortho_hbm, coeff_hbm, upper_hbm,
    k0, ke, diag, mass, velocities, shifts, sample,
    mat, xs, xh, yh, raw, applied, fields, data, full, packed, part, zpart, zsum, total, total_z,
    weights, result, coeff, upper,
    local_sems, b_send, b_recv, x_send, x_recv, y_send, y_recv, r_send, r_recv, o_sems,
):
    space, sides, plane, row_count = sizes
    depth = space // plane
    members = sides * plane
    share = 32 // members
    s = lax.axis_index("space")
    b = lax.axis_index("basis")
    z = s // plane
    spot = s - z * plane
    me = b * plane + spot

    def member(k):
        index = lax.rem(me + k, members)
        side = index // plane
        return index, (z * plane + (index - side * plane), side)

    def level(k):
        index = lax.rem(z + k, depth)
        return index, (index * plane + spot, b)

    small = [
        (sample_hbm, sample), (vel_hbm, velocities), (shift_hbm, shifts), (k0_hbm, k0),
        (ke_hbm, ke), (diag_hbm, diag), (mass_hbm, mass), (mat_hbm, mat),
        (x_hbm.at[:, :, 0], xs),
        (basis_hbm.at[:, :, 0, pl.ds(pl.multiple_of(b * 8, 8), 8), :], raw.at[b]),
    ]
    small = [
        pltpu.make_async_copy(source, target, local_sems.at[i])
        for i, (source, target) in enumerate(small)
    ]
    for copy in small:
        copy.start()

    barrier = pltpu.get_barrier_semaphore()

    def greet(peer):
        pl.semaphore_signal(barrier, inc=1, device_id=peer, device_id_type=MESH)

    @pl.loop(1, members)
    def _(k):
        greet(member(k)[1])

    @pl.loop(1, depth)
    def _(k):
        greet(level(k)[1])

    over = (spot == plane - 1) & (z < depth - 1)
    under = (spot == 0) & (z > 0)

    @pl.when(over)
    def _():
        greet((s + 1, b))

    @pl.when(under)
    def _():
        greet((s - 1, b))

    extra = jnp.where(over | under, 1, 0)
    pl.semaphore_wait(barrier, members + depth - 2 + extra)

    def remote(source, target, send, recv, peer):
        return pltpu.make_async_remote_copy(
            src_ref=source, dst_ref=target, send_sem=send, recv_sem=recv,
            device_id=peer, device_id_type=MESH,
        )

    def basis_copy(k):
        side = lax.rem(b + k, sides)
        return remote(
            basis_hbm.at[:, :, 0, pl.ds(pl.multiple_of(side * 8, 8), 8), :],
            raw.at[b], b_send.at[k - 1], b_recv.at[k - 1], (s, side),
        )

    def x_copy(way):
        peer = s + 1 if way == 0 else s - 1
        return remote(x_hbm.at[:, :, 0], xh.at[way], x_send.at[way], x_recv.at[way], (peer, b))

    def y_copy(way):
        peer = b + 1 if way == 0 else b - 1
        edge = 7 if way == 0 else 0
        return remote(
            x_hbm.at[:, :, 0, edge : edge + 1, :], yh.at[way], y_send.at[way], y_recv.at[way],
            (s, peer),
        )

    x_sends = [s < space - 1, s > 0]
    x_gets = [s > 0, s < space - 1]
    y_sends = [b < sides - 1, b > 0]
    y_gets = [b > 0, b < sides - 1]
    for way in range(2):
        pl.when(y_sends[way])(lambda way=way: y_copy(way).start())
    for k in (2, 1, 3):
        basis_copy(k).start()
    for way in range(2):
        pl.when(x_sends[way])(lambda way=way: x_copy(way).start())

    for copy in small[:8]:
        copy.wait()
    fill_fields(mat, k0, ke, diag, mass, velocities, shifts, sample, fields)
    small[9].wait()
    own = pl.multiple_of(b * 16, 16)
    split_rows(raw.at[b].reshape(384, 128), data, own)
    small[8].wait()

    for way in range(2):
        @pl.when(jnp.logical_not(x_gets[way]))
        def _():
            xh[way] = jnp.zeros(xs.shape, F32)

        @pl.when(jnp.logical_not(y_gets[way]))
        def _():
            yh[way] = jnp.zeros((16, 3, 1, 128), F32)

        pl.when(x_gets[way])(lambda way=way: x_copy(way).wait_recv())
        pl.when(y_gets[way])(lambda way=way: y_copy(way).wait_recv())

    apply_stencil(xs, xh, yh, fields, applied)
    split_rows(applied.reshape(384, 128), data, 64)

    for k in (1, 3, 2):
        basis_copy(k).wait_recv()
        side = lax.rem(b + sides - k, sides)
        split_rows(raw.at[side].reshape(384, 128), data, pl.multiple_of(side * 16, 16))

    products = lax.dot_general(
        data[...], data[...], (((1,), (1,)), ((), ())), preferred_element_type=F32
    )
    products = products[0:80] + products[80:160]
    full[:, 0:80] = products[:, 0:80] + products[:, 80:160]
    pack_upper(full, packed)

    def rows_of(index):
        return pl.ds(index * share, share)

    def scatter_copy(k):
        index, peer = member(k)
        return remote(
            packed.at[rows_of(index)], part.at[rows_of(me)], r_send.at[0], r_recv.at[0], peer
        )

    def level_copy(k):
        _, peer = level(k)
        return remote(zpart, zsum.at[rows_of(z)], r_send.at[1], r_recv.at[1], peer)

    def gather_copy(k):
        _, peer = member(k)
        return remote(total_z, total.at[rows_of(me)], r_send.at[2], r_recv.at[2], peer)

    def fold(ref, count):
        if share == 1:
            return jnp.sum(ref[...], axis=0, keepdims=True)
        return functools.reduce(
            lambda a, c: a + c, [ref[m * share : (m + 1) * share] for m in range(count)]
        )

    def wait_rows(ref, count, sem):
        view = ref.at[pl.ds(0, count * share)]
        pltpu.make_async_copy(view, view, sem).wait()

    @pl.loop(1, members)
    def _(k):
        scatter_copy(k).start()

    part[rows_of(me)] = packed[rows_of(me)]
    wait_rows(part, members - 1, r_recv.at[0])
    zpart[...] = fold(part, members)

    @pl.loop(1, depth)
    def _(k):
        level_copy(k).start()

    zsum[rows_of(z)] = zpart[...]
    wait_rows(zsum, depth - 1, r_recv.at[1])
    total_z[...] = fold(zsum, depth)

    @pl.loop(1, members)
    def _(k):
        gather_copy(k).start()

    total[rows_of(me)] = total_z[...]
    wait_rows(total, members - 1, r_recv.at[2])

    moments = unpack_full(total, 1.0 / row_count)
    lane64 = iota((64, 128), 1)
    first = jnp.where(lane64 < 16, pltpu.roll(moments[0:64], 64, 1), 0.0)
    gram_basis = jnp.where(lane64 < 64, moments[0:64], 0.0)
    zeros64 = jnp.zeros((64, 128), F32)
    both = 2.0 * first - dot_exact(gram_basis, jnp.concatenate([first, zeros64], axis=0))
    full[0:64, :] = both
    coeff[...] = full[pl.ds(own, 16), 0:16]
    coeff_out = pltpu.make_async_copy(coeff, coeff_hbm, o_sems.at[0])
    coeff_out.start()
    unit = jnp.where((iota((64, 128), 0) == lane64) & (lane64 < 16), 1.0, 0.0)
    mix = jnp.concatenate([-both, unit], axis=0)
    image = dot_exact(moments, mix)
    mix_t = mix.T[0:16]
    gram = dot_exact(mix_t, image)
    factors = factor(gram)
    upper[...] = jnp.where(iota((16, 16), 0) <= iota((16, 16), 1), factors[:, 0:16], 0.0)
    upper_out = pltpu.make_async_copy(upper, upper_hbm, o_sems.at[1])
    upper_out.start()
    inverse = pltpu.roll(factors, 112, 1)
    inverse = jnp.where(iota((16, 128), 1) < 16, inverse, 0.0)
    weight = dot_exact(
        inverse, jnp.concatenate([mix_t, jnp.zeros((112, 128), F32)], axis=0)
    )
    high = weight.astype(BF16).astype(F32)
    stacked = jnp.concatenate([high, weight - high], axis=0)
    weights[:, 0:80] = stacked[:, 0:80]
    weights[:, 80:160] = stacked[:, 0:80]
    left = weights[:, 0:160].astype(BF16)
    out = result.reshape(384, 128)
    for t in range(0, 24, 2):
        piece = jnp.dot(left, data[:, t * 128 : t * 128 + 256], preferred_element_type=F32)
        piece = piece[0:16] + piece[16:32]
        out[pl.ds(t, 16, stride=24), :] = piece[:, 0:128]
        out[pl.ds(t + 1, 16, stride=24), :] = piece[:, 128:256]
    ortho_out = pltpu.make_async_copy(result, ortho_hbm.at[:, :, 0], o_sems.at[2])
    ortho_out.start()

    for k in (1, 2, 3):
        basis_copy(k).wait_send()
    for way in range(2):
        pl.when(x_sends[way])(lambda way=way: x_copy(way).wait_send())
        pl.when(y_sends[way])(lambda way=way: y_copy(way).wait_send())
    wait_rows(part, members - 1, r_send.at[0])
    wait_rows(zsum, depth - 1, r_send.at[1])
    wait_rows(total, members - 1, r_send.at[2])
    coeff_out.wait()
    upper_out.wait()
    ortho_out.wait()


def shards(space, sides, x_block, basis, material, k0, diag, ke, mass, velocities, shifts, sample):
    plane = PLANE
    share = 32 // (sides * plane)
    depth = space // plane
    row_count = 3.0 * space * x_block.shape[3] * sides * x_block.shape[4]
    vmem, smem, dma = pltpu.VMEM, pltpu.SMEM, pltpu.SemaphoreType.DMA
    block = (16, 3, 8, 128)
    scratch = [
        smem((3, 3, 8, 7), F32), smem((3, 3, 8, 7), F32), smem((3, 8), F32), smem((3, 8), F32),
        smem((8, 128), F32), smem((8, 128), F32), smem((1, 1), jnp.int32),
        vmem((1, 8, 128), jnp.int32), vmem(block, F32), vmem((2,) + block, F32),
        vmem((2, 16, 3, 1, 128), F32), vmem((sides,) + block, F32), vmem(block, F32),
        vmem((63, 8, 128), F32), vmem((160, 3072), BF16), vmem((80, 128), F32),
        vmem((32, 128), F32), vmem((32, 128), F32), vmem((share, 128), F32),
        vmem((depth * share, 128), F32), vmem((32, 128), F32), vmem((share, 128), F32),
        vmem((32, 256), F32), vmem(block, F32), vmem((16, 16), F32), vmem((16, 16), F32),
        dma((10,)), dma((3,)), dma((3,)), dma((2,)), dma((2,)), dma((2,)), dma((2,)),
        dma((3,)), dma((3,)), dma((3,)),
    ]
    whole = pl.BlockSpec(memory_space=pltpu.HBM)
    return pl.pallas_call(
        functools.partial(kernel, (space, sides, plane, row_count)),
        out_shape=(
            jax.ShapeDtypeStruct(x_block.shape, F32),
            jax.ShapeDtypeStruct((16, 16), F32),
            jax.ShapeDtypeStruct((16, 16), F32),
        ),
        in_specs=[whole] * 10,
        out_specs=(whole,) * 3,
        scratch_shapes=scratch,
        compiler_params=pltpu.CompilerParams(
            collective_id=0, has_side_effects=True, vmem_limit_bytes=64 * 1024 * 1024
        ),
    )(
        x_block, basis, material,
        jnp.transpose(k0, (2, 3, 0, 1)), jnp.transpose(ke, (2, 3, 0, 1)),
        diag.T, mass.T, velocities.reshape(8, 128), shifts.reshape(8, 128), sample.reshape(1, 1),
    )


def solution(mesh):
    in_specs = (
        P(None, None, "space", "basis", None), P("basis", None, "space", None, None),
        P("space", "basis", None), P(), P(), P(), P(), P(), P(), P(),
    )
    out_specs = (P(None, None, "space", "basis", None), P("basis", None), P())
    body = functools.partial(shards, mesh.shape["space"], mesh.shape["basis"])
    return jax.shard_map(body, mesh=mesh, in_specs=in_specs, out_specs=out_specs, check_vma=False)
```

```python
import functools

import jax
import jax.numpy as jnp
from jax import lax
from jax.experimental import pallas as pl
from jax.experimental.pallas import tpu as pltpu
from jax.sharding import PartitionSpec as P

MESH = pl.DeviceIdType.MESH
PLANE = 8
EXACT = lax.Precision.HIGHEST
F32 = jnp.float32
BF16 = jnp.bfloat16


def dot_exact(a, b):
    return lax.dot_general(
        a, b, (((1,), (0,)), ((), ())), precision=EXACT, preferred_element_type=F32
    )


def iota(shape, axis):
    return lax.broadcasted_iota(jnp.int32, shape, axis)


def pick(bits, values):
    level = list(values)
    for bit in bits:
        level = [jnp.where(bit, level[i + 1], level[i]) for i in range(0, len(level), 2)]
    return level[0]


def fill_fields(mat_ref, k0, ke, diag, mass, velocities, shifts, sample, fields):
    index = sample[0]
    velocity = velocities[index // 128, index % 128]
    shift = shifts[index // 128, index % 128]
    square = velocity * velocity
    cells = mat_ref[0]
    bits = [((cells >> b) & 1) == 1 for b in range(3)]

    def offset_body(o, carry):
        for i in range(3):
            for j in range(3):
                values = [k0[i, j, m, o] - square * ke[i, j, m, o] for m in range(8)]
                fields[o * 9 + i * 3 + j] = pick(bits, values)
        return carry

    lax.fori_loop(0, 7, offset_body, 0)
    for i in range(3):
        values = [diag[i, m] - shift * mass[i, m] for m in range(8)]
        fields[4 * i] = fields[4 * i] + pick(bits, values)


def apply_stencil(xs, xh, yh, fields, applied):
    row = iota((8, 128), 0)
    lane = iota((8, 128), 1)

    def column(n, carry):
        sums = [None] * 3
        for j in range(3):
            centre = xs[n, j]
            low_y = jnp.where(
                row == 0, jnp.broadcast_to(yh[0, n, j], (8, 128)), pltpu.roll(centre, 1, 0)
            )
            high_y = jnp.where(
                row == 7, jnp.broadcast_to(yh[1, n, j], (8, 128)), pltpu.roll(centre, 7, 0)
            )
            low_z = jnp.where(lane == 0, 0.0, pltpu.roll(centre, 1, 1))
            high_z = jnp.where(lane == 127, 0.0, pltpu.roll(centre, 127, 1))
            views = [centre, xh[0, n, j], xh[1, n, j], low_y, high_y, low_z, high_z]
            for o in range(7):
                for i in range(3):
                    term = fields[o * 9 + i * 3 + j] * views[o]
                    sums[i] = term if sums[i] is None else sums[i] + term
        for i in range(3):
            applied[n, i] = sums[i]
        return carry

    lax.fori_loop(0, 16, column, 0)


def split_rows(raw, data, first, part):
    def tile(i, carry):
        t = part * 8 + i
        block = raw[pl.ds(t, 16, stride=24), :]
        high = block.astype(BF16)
        rest = (block - high.astype(F32)).astype(BF16)
        lanes = pl.ds(pl.multiple_of(t * 128, 128), 128)
        data[pl.ds(first, 16), lanes] = high
        data[pl.ds(80 + first, 16), lanes] = rest
        return carry

    lax.fori_loop(0, 8, tile, 0, unroll=True)


def pack_upper(full, packed):
    lane = iota((16, 128), 1)
    rows = [full[16 * g : 16 * g + 16, :] for g in range(5)]
    packed[0:16, :] = jnp.where(lane < 80, rows[0], pltpu.roll(rows[2], 48, 1))
    packed[16:32, :] = jnp.where(
        lane < 64,
        pltpu.roll(rows[1], 112, 1),
        jnp.where(
            lane < 96,
            pltpu.roll(rows[3], 16, 1),
            jnp.where(lane < 112, pltpu.roll(rows[4], 32, 1), 0.0),
        ),
    )


def unpack_full(packed, scale):
    lane = iota((16, 128), 1)
    one, two = packed[0:16, :], packed[16:32, :]
    parts = [
        one,
        pltpu.roll(two, 16, 1),
        pltpu.roll(one, 80, 1),
        pltpu.roll(two, 112, 1),
        pltpu.roll(two, 96, 1),
    ]
    rows = []
    for g in range(5):
        weight = jnp.where(lane < 16 * g + 16, 0.5 * scale, scale)
        rows.append(jnp.where((lane >= 16 * g) & (lane < 80), parts[g] * weight, 0.0))
    rows.append(jnp.zeros((48, 128), F32))
    upper = jnp.concatenate(rows, axis=0)
    return upper + upper.T


def factor(gram):
    row = iota((16, 128), 0)
    lane = iota((16, 128), 1)
    work = jnp.where(lane < 16, gram, jnp.where(lane == row + 16, 1.0, 0.0))
    for k in range(15):
        pivot_row = jnp.broadcast_to(work[k : k + 1, :], (16, 128))
        column = jnp.broadcast_to(work[:, k : k + 1], (16, 128))
        pivot = jnp.broadcast_to(work[k : k + 1, k : k + 1], (16, 128))
        work = work - jnp.where(row > k, column / pivot, 0.0) * pivot_row
    pivots = jnp.sum(jnp.where(lane == row, work, 0.0), axis=1, keepdims=True)
    root = lax.rsqrt(pivots)
    root = root * (1.5 - 0.5 * pivots * root * root)
    return work * root


def kernel(
    sizes,
    x_hbm, basis_hbm, mat_hbm, k0_hbm, ke_hbm, diag_hbm, mass_hbm, vel_hbm, shift_hbm, sample,
    total, data_hbm,
    k0, ke, diag, mass, velocities, shifts,
    mat, xs, xh, yh, raw, applied, fields, data, full, packed, part, zpart, zsum, total_z,
    local_sems, b_send, b_recv, x_send, x_recv, y_send, y_recv, r_send, r_recv, o_sems,
):
    space, sides, plane, row_count = sizes
    depth = space // plane
    members = sides * plane
    share = 32 // members
    lines = plane // 2
    s = lax.axis_index("space")
    b = lax.axis_index("basis")
    z = s // plane
    spot = s - z * plane
    x = spot // 2
    core = spot - 2 * x
    me = b * plane + spot

    def members_each(act):
        sites = [(dx, dy) for dx in range(lines) for dy in range(sides)]
        sites.sort(key=lambda d: -(min(d[0], lines - d[0]) + min(d[1], sides - d[1])))
        for dx, dy in sites:
            column, side = lax.rem(x + dx, lines), lax.rem(b + dy, sides)
            for other in ((1 - core, core) if dx or dy else (1 - core,)):
                index = side * plane + column * 2 + other
                act(index, (z * plane + column * 2 + other, side))

    def levels_each(act):
        far = depth // 2
        act((lax.rem(z + far, depth) * plane + spot, b))
        for d in range(far - 1, 0, -1):
            act((lax.rem(z + d, depth) * plane + spot, b))
            act((lax.rem(z + depth - d, depth) * plane + spot, b))

    barrier = pltpu.get_barrier_semaphore()

    def greet(peer):
        pl.semaphore_signal(barrier, inc=1, device_id=peer, device_id_type=MESH)

    over = (spot == plane - 1) & (z < depth - 1)
    under = (spot == 0) & (z > 0)
    levels_each(greet)

    @pl.when(over | under)
    def _():
        greet((jnp.where(over, s + 1, s - 1), b))

    members_each(lambda index, peer: greet(peer))

    small = [
        (vel_hbm, velocities), (shift_hbm, shifts), (k0_hbm, k0),
        (ke_hbm, ke), (diag_hbm, diag), (mass_hbm, mass), (mat_hbm, mat),
        (x_hbm.at[:, :, 0], xs),
        (basis_hbm.at[:, :, 0, pl.ds(pl.multiple_of(b * 8, 8), 8), :], raw.at[b]),
    ]
    small = [
        pltpu.make_async_copy(source, target, local_sems.at[i])
        for i, (source, target) in enumerate(small)
    ]
    for copy in small:
        copy.start()

    extra = jnp.where(over | under, 1, 0)
    pl.semaphore_wait(barrier, members + depth - 2 + extra)

    def remote(source, target, send, recv, peer):
        return pltpu.make_async_remote_copy(
            src_ref=source, dst_ref=target, send_sem=send, recv_sem=recv,
            device_id=peer, device_id_type=MESH,
        )

    def basis_copy(k, c):
        side = lax.rem(b + k, sides)
        return remote(
            basis_hbm.at[:, c, 0, pl.ds(pl.multiple_of(side * 8, 8), 8), :],
            raw.at[b, :, c], b_send.at[k - 1, c], b_recv.at[k - 1, c], (s, side),
        )

    def x_copy(way):
        peer = s + 1 if way == 0 else s - 1
        return remote(x_hbm.at[:, :, 0], xh.at[way], x_send.at[way], x_recv.at[way], (peer, b))

    def y_copy(way):
        peer = b + 1 if way == 0 else b - 1
        edge = 7 if way == 0 else 0
        return remote(
            x_hbm.at[:, :, 0, edge : edge + 1, :], yh.at[way], y_send.at[way], y_recv.at[way],
            (s, peer),
        )

    x_sends = [s < space - 1, s > 0]
    x_gets = [s > 0, s < space - 1]
    y_sends = [b < sides - 1, b > 0]
    y_gets = [b > 0, b < sides - 1]
    for way in range(2):
        pl.when(y_sends[way])(lambda way=way: y_copy(way).start())
    for c in range(3):
        for k in (2, 1, 3):
            basis_copy(k, c).start()
    for way in range(2):
        pl.when(x_sends[way])(lambda way=way: x_copy(way).start())

    for copy in small[:7]:
        copy.wait()
    fill_fields(mat, k0, ke, diag, mass, velocities, shifts, sample, fields)
    small[8].wait()
    own = pl.multiple_of(b * 16, 16)
    for c in range(3):
        split_rows(raw.at[b].reshape(384, 128), data, own, c)
    small[7].wait()

    for way in range(2):
        @pl.when(jnp.logical_not(x_gets[way]))
        def _():
            xh[way] = jnp.zeros(xs.shape, F32)

        @pl.when(jnp.logical_not(y_gets[way]))
        def _():
            yh[way] = jnp.zeros((16, 3, 1, 128), F32)

        pl.when(x_gets[way])(lambda way=way: x_copy(way).wait_recv())
        pl.when(y_gets[way])(lambda way=way: y_copy(way).wait_recv())

    apply_stencil(xs, xh, yh, fields, applied)
    for c in range(3):
        split_rows(applied.reshape(384, 128), data, 64, c)

    products = None
    for c in range(3):
        for k in (1, 3, 2):
            basis_copy(k, c).wait_recv()
            side = lax.rem(b + sides - k, sides)
            split_rows(raw.at[side].reshape(384, 128), data, pl.multiple_of(side * 16, 16), c)
        piece = data[:, c * 1024 : (c + 1) * 1024]
        term = lax.dot_general(
            piece, piece, (((1,), (1,)), ((), ())), preferred_element_type=F32
        )
        products = term if products is None else products + term
    products = products[0:80] + products[80:160]
    full[:, 0:80] = products[:, 0:80] + products[:, 80:160]
    pack_upper(full, packed)

    data_out = pltpu.make_async_copy(data, data_hbm, o_sems.at[0])
    data_out.start()

    def rows_of(index):
        return pl.ds(index * share, share)

    def scatter(index, peer):
        remote(
            packed.at[rows_of(index)], part.at[rows_of(me)], r_send.at[0], r_recv.at[0], peer
        ).start()

    def along(peer):
        remote(zpart, zsum.at[rows_of(z)], r_send.at[1], r_recv.at[1], peer).start()

    def gather(index, peer):
        remote(total_z, total.at[rows_of(me)], r_send.at[2], r_recv.at[2], peer).start()

    def fold(ref, count):
        if share == 1:
            return jnp.sum(ref[...], axis=0, keepdims=True)
        return functools.reduce(
            lambda a, c: a + c, [ref[m * share : (m + 1) * share] for m in range(count)]
        )

    def wait_rows(ref, count, sem):
        view = ref.at[pl.ds(0, count * share)]
        pltpu.make_async_copy(view, view, sem).wait()

    members_each(scatter)
    part[rows_of(me)] = packed[rows_of(me)]
    wait_rows(part, members - 1, r_recv.at[0])
    zpart[...] = fold(part, members)
    levels_each(along)
    zsum[rows_of(z)] = zpart[...]
    wait_rows(zsum, depth - 1, r_recv.at[1])
    total_z[...] = fold(zsum, depth)
    members_each(gather)
    own_rows = pltpu.make_async_copy(total_z, total.at[rows_of(me)], o_sems.at[1])
    own_rows.start()
    wait_rows(total, members - 1, r_recv.at[2])
    own_rows.wait()
    data_out.wait()
    for c in range(3):
        for k in (1, 2, 3):
            basis_copy(k, c).wait_send()
    for way in range(2):
        pl.when(x_sends[way])(lambda way=way: x_copy(way).wait_send())
        pl.when(y_sends[way])(lambda way=way: y_copy(way).wait_send())
    wait_rows(part, members - 1, r_send.at[0])
    wait_rows(zsum, depth - 1, r_send.at[1])
    wait_rows(total, members - 1, r_send.at[2])


def finish(
    row_count,
    total_hbm, data_hbm, ortho_hbm, coeff_hbm, upper_hbm,
    total, data, full, weights, result, coeff, upper, i_sems, o_sems,
):
    total_in = pltpu.make_async_copy(total_hbm, total, i_sems.at[0])
    total_in.start()
    data_in = pltpu.make_async_copy(data_hbm, data, i_sems.at[1])
    data_in.start()
    own = pl.multiple_of(lax.axis_index("basis") * 16, 16)

    total_in.wait()
    moments = unpack_full(total, 1.0 / row_count)
    lane64 = iota((64, 128), 1)
    first = jnp.where(lane64 < 16, pltpu.roll(moments[0:64], 64, 1), 0.0)
    gram_basis = jnp.where(lane64 < 64, moments[0:64], 0.0)
    zeros64 = jnp.zeros((64, 128), F32)
    both = 2.0 * first - dot_exact(gram_basis, jnp.concatenate([first, zeros64], axis=0))
    full[0:64, :] = both
    coeff[...] = full[pl.ds(own, 16), 0:16]
    coeff_out = pltpu.make_async_copy(coeff, coeff_hbm, o_sems.at[0])
    coeff_out.start()
    unit = jnp.where((iota((64, 128), 0) == lane64) & (lane64 < 16), 1.0, 0.0)
    mix = jnp.concatenate([-both, unit], axis=0)
    image = dot_exact(moments, mix)
    mix_t = mix.T[0:16]
    gram = dot_exact(mix_t, image)
    factors = factor(gram)
    upper[...] = jnp.where(iota((16, 16), 0) <= iota((16, 16), 1), factors[:, 0:16], 0.0)
    upper_out = pltpu.make_async_copy(upper, upper_hbm, o_sems.at[1])
    upper_out.start()
    inverse = pltpu.roll(factors, 112, 1)
    inverse = jnp.where(iota((16, 128), 1) < 16, inverse, 0.0)
    weight = dot_exact(
        inverse, jnp.concatenate([mix_t, jnp.zeros((112, 128), F32)], axis=0)
    )
    high = weight.astype(BF16).astype(F32)
    stacked = jnp.concatenate([high, weight - high], axis=0)
    weights[:, 0:80] = stacked[:, 0:80]
    weights[:, 80:160] = stacked[:, 0:80]
    data_in.wait()
    left = weights[:, 0:160].astype(BF16)
    out = result.reshape(384, 128)
    for t in range(0, 24, 2):
        piece = jnp.dot(left, data[:, t * 128 : t * 128 + 256], preferred_element_type=F32)
        piece = piece[0:16] + piece[16:32]
        out[pl.ds(t, 16, stride=24), :] = piece[:, 0:128]
        out[pl.ds(t + 1, 16, stride=24), :] = piece[:, 128:256]
    ortho_out = pltpu.make_async_copy(result, ortho_hbm.at[:, :, 0], o_sems.at[2])
    ortho_out.start()
    coeff_out.wait()
    upper_out.wait()
    ortho_out.wait()


def shards(space, sides, x_block, basis, material, k0, diag, ke, mass, velocities, shifts, sample):
    plane = PLANE
    share = 32 // (sides * plane)
    depth = space // plane
    row_count = 3.0 * space * x_block.shape[3] * sides * x_block.shape[4]
    vmem, smem, dma = pltpu.VMEM, pltpu.SMEM, pltpu.SemaphoreType.DMA
    block = (16, 3, 8, 128)
    scratch = [
        smem((3, 3, 8, 7), F32), smem((3, 3, 8, 7), F32), smem((3, 8), F32), smem((3, 8), F32),
        smem((8, 128), F32), smem((8, 128), F32),
        vmem((1, 8, 128), jnp.int32), vmem(block, F32), vmem((2,) + block, F32),
        vmem((2, 16, 3, 1, 128), F32), vmem((sides,) + block, F32), vmem(block, F32),
        vmem((63, 8, 128), F32), vmem((160, 3072), BF16), vmem((80, 128), F32),
        vmem((32, 128), F32), vmem((32, 128), F32), vmem((share, 128), F32),
        vmem((depth * share, 128), F32), vmem((share, 128), F32),
        dma((9,)), dma((3, 3)), dma((3, 3)), dma((2,)), dma((2,)), dma((2,)), dma((2,)),
        dma((3,)), dma((3,)), dma((2,)),
    ]
    whole = pl.BlockSpec(memory_space=pltpu.HBM)
    outs = pl.pallas_call(
        functools.partial(kernel, (space, sides, plane, row_count)),
        out_shape=(
            jax.ShapeDtypeStruct((32, 128), F32),
            jax.ShapeDtypeStruct((160, 3072), BF16),
        ),
        in_specs=[whole] * 9 + [pl.BlockSpec(memory_space=smem)],
        out_specs=(whole,) * 2,
        scratch_shapes=scratch,
        compiler_params=pltpu.CompilerParams(
            collective_id=0, has_side_effects=True, vmem_limit_bytes=64 * 1024 * 1024
        ),
    )(
        x_block, basis, material,
        jnp.transpose(k0, (2, 3, 0, 1)), jnp.transpose(ke, (2, 3, 0, 1)),
        diag.T, mass.T, velocities.reshape(8, 128), shifts.reshape(8, 128), sample,
    )
    return pl.pallas_call(
        functools.partial(finish, row_count),
        out_shape=(
            jax.ShapeDtypeStruct(x_block.shape, F32),
            jax.ShapeDtypeStruct((16, 16), F32),
            jax.ShapeDtypeStruct((16, 16), F32),
        ),
        in_specs=[whole] * 2,
        out_specs=(whole,) * 3,
        scratch_shapes=[
            vmem((32, 128), F32), vmem((160, 3072), BF16), vmem((80, 128), F32),
            vmem((32, 256), F32), vmem(block, F32), vmem((16, 16), F32), vmem((16, 16), F32),
            dma((2,)), dma((3,)),
        ],
        compiler_params=pltpu.CompilerParams(vmem_limit_bytes=64 * 1024 * 1024),
    )(*outs)


def solution(mesh):
    in_specs = (
        P(None, None, "space", "basis", None), P("basis", None, "space", None, None),
        P("space", "basis", None), P(), P(), P(), P(), P(), P(), P(),
    )
    out_specs = (P(None, None, "space", "basis", None), P("basis", None), P())
    body = functools.partial(shards, mesh.shape["space"], mesh.shape["basis"])
    return jax.shard_map(body, mesh=mesh, in_specs=in_specs, out_specs=out_specs, check_vma=False)
```

```python
import functools

import jax
import jax.numpy as jnp
from jax import lax
from jax.experimental import pallas as pl
from jax.experimental.pallas import tpu as pltpu
from jax.sharding import PartitionSpec as P

MESH = pl.DeviceIdType.MESH
PLANE = 8
HOLDERS = 2
EXACT = lax.Precision.HIGHEST
F32 = jnp.float32
BF16 = jnp.bfloat16


def dot_exact(a, b):
    return lax.dot_general(
        a, b, (((1,), (0,)), ((), ())), precision=EXACT, preferred_element_type=F32
    )


def iota(shape, axis):
    return lax.broadcasted_iota(jnp.int32, shape, axis)


def pick(bits, values):
    level = list(values)
    for bit in bits:
        level = [jnp.where(bit, level[i + 1], level[i]) for i in range(0, len(level), 2)]
    return level[0]


def fill_fields(mat_ref, k0, ke, diag, mass, velocities, shifts, sample, fields):
    index = sample[0]
    velocity = velocities[index // 128, index % 128]
    shift = shifts[index // 128, index % 128]
    square = velocity * velocity
    cells = mat_ref[0]
    bits = [((cells >> b) & 1) == 1 for b in range(3)]

    def offset_body(o, carry):
        for i in range(3):
            for j in range(3):
                values = [k0[i, j, m, o] - square * ke[i, j, m, o] for m in range(8)]
                fields[o * 9 + i * 3 + j] = pick(bits, values)
        return carry

    lax.fori_loop(0, 7, offset_body, 0)
    for i in range(3):
        values = [diag[i, m] - shift * mass[i, m] for m in range(8)]
        fields[4 * i] = fields[4 * i] + pick(bits, values)


def apply_stencil(xs, xh, yh, fields, applied):
    row = iota((8, 128), 0)
    lane = iota((8, 128), 1)

    def column(n, carry):
        sums = [None] * 3
        for j in range(3):
            centre = xs[n, j]
            low_y = jnp.where(
                row == 0, jnp.broadcast_to(yh[0, n, j], (8, 128)), pltpu.roll(centre, 1, 0)
            )
            high_y = jnp.where(
                row == 7, jnp.broadcast_to(yh[1, n, j], (8, 128)), pltpu.roll(centre, 7, 0)
            )
            low_z = jnp.where(lane == 0, 0.0, pltpu.roll(centre, 1, 1))
            high_z = jnp.where(lane == 127, 0.0, pltpu.roll(centre, 127, 1))
            views = [centre, xh[0, n, j], xh[1, n, j], low_y, high_y, low_z, high_z]
            for o in range(7):
                for i in range(3):
                    term = fields[o * 9 + i * 3 + j] * views[o]
                    sums[i] = term if sums[i] is None else sums[i] + term
        for i in range(3):
            applied[n, i] = sums[i]
        return carry

    lax.fori_loop(0, 16, column, 0)


def split_rows(raw, data, first, part):
    def tile(i, carry):
        t = part * 8 + i
        block = raw[pl.ds(t, 16, stride=24), :]
        high = block.astype(BF16)
        rest = (block - high.astype(F32)).astype(BF16)
        lanes = pl.ds(pl.multiple_of(t * 128, 128), 128)
        data[pl.ds(first, 16), lanes] = high
        data[pl.ds(80 + first, 16), lanes] = rest
        return carry

    lax.fori_loop(0, 8, tile, 0, unroll=True)


def pack_upper(full, packed):
    lane = iota((16, 128), 1)
    rows = [full[16 * g : 16 * g + 16, :] for g in range(5)]
    packed[0:16, :] = jnp.where(lane < 80, rows[0], pltpu.roll(rows[2], 48, 1))
    packed[16:32, :] = jnp.where(
        lane < 64,
        pltpu.roll(rows[1], 112, 1),
        jnp.where(
            lane < 96,
            pltpu.roll(rows[3], 16, 1),
            jnp.where(lane < 112, pltpu.roll(rows[4], 32, 1), 0.0),
        ),
    )


def unpack_full(packed, scale):
    lane = iota((16, 128), 1)
    one, two = packed[0:16, :], packed[16:32, :]
    parts = [
        one,
        pltpu.roll(two, 16, 1),
        pltpu.roll(one, 80, 1),
        pltpu.roll(two, 112, 1),
        pltpu.roll(two, 96, 1),
    ]
    rows = []
    for g in range(5):
        weight = jnp.where(lane < 16 * g + 16, 0.5 * scale, scale)
        rows.append(jnp.where((lane >= 16 * g) & (lane < 80), parts[g] * weight, 0.0))
    rows.append(jnp.zeros((48, 128), F32))
    upper = jnp.concatenate(rows, axis=0)
    return upper + upper.T


def factor(gram, spread, lines):
    lane = iota((8, 128), 1)
    for j in range(16):
        spread[16 * j : 16 * j + 16, :] = jnp.broadcast_to(gram[:, j : j + 1], (16, 128))
    lines[...] = gram

    def full(ref, r):
        return jnp.broadcast_to(ref[r : r + 1, :], (8, 128))

    entry = {(i, j): full(spread, 16 * j + i) for j in range(16) for i in range(j, 16)}
    rows = [
        jnp.where(lane < 16, full(lines, i), jnp.where(lane == 16 + i, 1.0, 0.0))
        for i in range(16)
    ]
    for k in range(16):
        pivot = entry[k, k]
        inverse = 1.0 / pivot
        for i in range(k + 1, 16):
            scale = entry[i, k] * inverse
            for j in range(k + 1, i + 1):
                entry[i, j] = entry[i, j] - scale * entry[j, k]
            rows[i] = rows[i] - scale * rows[k]
        root = lax.rsqrt(pivot)
        root = root * (1.5 - 0.5 * pivot * root * root)
        lines[k : k + 1, :] = (rows[k] * root)[0:1]
    return lines[...]


def kernel(
    sizes,
    x_hbm, basis_hbm, mat_hbm, k0_hbm, ke_hbm, diag_hbm, mass_hbm, vel_hbm, shift_hbm, sample,
    total, data_hbm,
    k0, ke, diag, mass, velocities, shifts,
    mat, xs, xh, yh, whole, raw, applied, fields, data, full, packed, part, zpart, zsum, total_z,
    local_sems, b_send, b_recv, x_send, x_recv, y_send, y_recv, r_send, r_recv, o_sems, ready,
):
    space, sides, plane, row_count = sizes
    depth = space // plane
    lines = plane // 2
    members = sides * 2
    share = 32 // members
    s = lax.axis_index("space")
    b = lax.axis_index("basis")
    z = s // plane
    spot = s - z * plane
    x = spot // 2
    core = spot - 2 * x
    me = b * 2 + core
    place = z * lines + x
    holder = z < HOLDERS
    turn = depth // 2 + 1
    served = jnp.where(z < turn, 1, 0)
    clients = [range(turn, depth), range(HOLDERS, turn)]

    def members_each(act):
        sites = sorted(range(sides), key=lambda d: -min(d, sides - d))
        for dy in sites:
            side = lax.rem(b + dy, sides)
            for other in ((1 - core, core) if dy else (1 - core,)):
                act(side * 2 + other, (z * plane + x * 2 + other, side))

    def spot_at(level, column):
        return level * plane + column * 2 + core, b

    def holders_each(act):
        for level in range(HOLDERS):
            for column in range(lines):
                pl.when(place != level * lines + column)(
                    lambda level=level, column=column: act(spot_at(level, column))
                )

    barrier = pltpu.get_barrier_semaphore()

    def greet(peer):
        pl.semaphore_signal(barrier, inc=1, device_id=peer, device_id_type=MESH)

    beside = s + 2 * core - 1
    has_beside = (beside >= 0) & (beside < space)
    members_each(lambda index, peer: greet(peer))

    @pl.when(has_beside)
    def _():
        greet((beside, b))

    @pl.when(holder)
    def _():
        for level in range(HOLDERS):
            for column in range(lines):
                pl.when(place != level * lines + column)(
                    lambda level=level, column=column: greet(spot_at(level, column))
                )

        @pl.loop(HOLDERS, depth)
        def _(level):
            for column in range(lines):
                greet(spot_at(level, column))

    small = [
        (vel_hbm, velocities), (shift_hbm, shifts), (k0_hbm, k0),
        (ke_hbm, ke), (diag_hbm, diag), (mass_hbm, mass), (mat_hbm, mat),
        (basis_hbm.at[:, :, 0], whole), (x_hbm.at[:, :, 0], xs),
        (basis_hbm.at[:, :, 0, pl.ds(pl.multiple_of(b * 8, 8), 8), :], raw.at[b]),
    ]
    small = [
        pltpu.make_async_copy(source, target, local_sems.at[i])
        for i, (source, target) in enumerate(small)
    ]
    for copy in small:
        copy.start()

    known = members - 1 + HOLDERS * lines
    known = known + jnp.where(has_beside, 1, 0) - jnp.where(holder, 1, 0)
    pl.semaphore_wait(barrier, known)

    @pl.when(jnp.logical_not(holder))
    def _():
        pl.semaphore_signal(
            ready, inc=1, device_id=spot_at(served, x), device_id_type=MESH
        )

    def remote(source, target, send, recv, peer):
        return pltpu.make_async_remote_copy(
            src_ref=source, dst_ref=target, send_sem=send, recv_sem=recv,
            device_id=peer, device_id_type=MESH,
        )

    def basis_copy(k, c):
        side = lax.rem(b + k, sides)
        return remote(
            whole.at[:, c, pl.ds(pl.multiple_of(side * 8, 8), 8), :],
            raw.at[b, :, c], b_send.at[k - 1, c], b_recv.at[k - 1, c], (s, side),
        )

    def x_copy(way):
        peer = s + 1 if way == 0 else s - 1
        return remote(x_hbm.at[:, :, 0], xh.at[way], x_send.at[way], x_recv.at[way], (peer, b))

    def y_copy(way):
        peer = b + 1 if way == 0 else b - 1
        edge = 7 if way == 0 else 0
        return remote(
            x_hbm.at[:, :, 0, edge : edge + 1, :], yh.at[way], y_send.at[way], y_recv.at[way],
            (s, peer),
        )

    x_sends = [s < space - 1, s > 0]
    x_gets = [s > 0, s < space - 1]
    y_sends = [b < sides - 1, b > 0]
    y_gets = [b > 0, b < sides - 1]
    for way in range(2):
        pl.when(y_sends[way])(lambda way=way: y_copy(way).start())
    small[7].wait()
    for c in range(3):
        for k in (2, 1, 3):
            basis_copy(k, c).start()
    for way in range(2):
        pl.when(x_sends[way])(lambda way=way: x_copy(way).start())

    for copy in small[:7]:
        copy.wait()
    fill_fields(mat, k0, ke, diag, mass, velocities, shifts, sample, fields)
    small[9].wait()
    own = pl.multiple_of(b * 16, 16)
    for c in range(3):
        split_rows(raw.at[b].reshape(384, 128), data, own, c)
    small[8].wait()

    for way in range(2):
        @pl.when(jnp.logical_not(x_gets[way]))
        def _():
            xh[way] = jnp.zeros(xs.shape, F32)

        @pl.when(jnp.logical_not(y_gets[way]))
        def _():
            yh[way] = jnp.zeros((16, 3, 1, 128), F32)

        pl.when(x_gets[way])(lambda way=way: x_copy(way).wait_recv())
        pl.when(y_gets[way])(lambda way=way: y_copy(way).wait_recv())

    apply_stencil(xs, xh, yh, fields, applied)
    for c in range(3):
        split_rows(applied.reshape(384, 128), data, 64, c)

    products = None
    for c in range(3):
        for k in (1, 3, 2):
            basis_copy(k, c).wait_recv()
            side = lax.rem(b + sides - k, sides)
            split_rows(raw.at[side].reshape(384, 128), data, pl.multiple_of(side * 16, 16), c)
        piece = data[:, c * 1024 : (c + 1) * 1024]
        term = lax.dot_general(
            piece, piece, (((1,), (1,)), ((), ())), preferred_element_type=F32
        )
        products = term if products is None else products + term
    products = products[0:80] + products[80:160]
    full[:, 0:80] = products[:, 0:80] + products[:, 80:160]
    pack_upper(full, packed)

    def rows_of(index):
        return pl.ds(index * share, share)

    def scatter(index, peer):
        remote(
            packed.at[rows_of(index)], part.at[rows_of(me)], r_send.at[0], r_recv.at[0], peer
        ).start()

    def to_holder(peer):
        remote(zpart, zsum.at[rows_of(place)], r_send.at[1], r_recv.at[1], peer).start()

    def to_client(level):
        remote(total_z, total_z, r_send.at[3], r_recv.at[3], spot_at(level, x)).start()

    def gather(index, peer):
        remote(total_z, total.at[rows_of(me)], r_send.at[2], r_recv.at[2], peer).start()

    def fold(ref, count):
        tiles = [ref[8 * i : 8 * i + 8] for i in range(count * share // 8)]
        while len(tiles) > 1:
            half = (len(tiles) + 1) // 2
            tiles = [
                tiles[i] + tiles[i + half] if i + half < len(tiles) else tiles[i]
                for i in range(half)
            ]
        return tiles[0][0:4] + tiles[0][4:8]

    def wait_rows(ref, count, sem):
        view = ref.at[pl.ds(0, count * share)]
        pltpu.make_async_copy(view, view, sem).wait()

    members_each(scatter)
    part[rows_of(me)] = packed[rows_of(me)]
    data_out = pltpu.make_async_copy(data, data_hbm, o_sems.at[0])
    data_out.start()
    wait_rows(part, members - 1, r_recv.at[0])
    zpart[...] = fold(part, members)
    holders_each(to_holder)

    @pl.when(holder)
    def _():
        zsum[rows_of(place)] = zpart[...]
        wait_rows(zsum, depth * lines - 1, r_recv.at[1])
        total_z[...] = fold(zsum, depth * lines)

    for level in range(HOLDERS):
        @pl.when(z == level)
        def _():
            pl.semaphore_wait(ready, len(clients[level]))
            for client in clients[level]:
                to_client(client)

    @pl.when(jnp.logical_not(holder))
    def _():
        wait_rows(total_z, 1, r_recv.at[3])

    members_each(gather)
    own_rows = pltpu.make_async_copy(total_z, total.at[rows_of(me)], o_sems.at[1])
    own_rows.start()
    wait_rows(total, members - 1, r_recv.at[2])
    own_rows.wait()
    data_out.wait()
    for c in range(3):
        for k in (1, 2, 3):
            basis_copy(k, c).wait_send()
    for way in range(2):
        pl.when(x_sends[way])(lambda way=way: x_copy(way).wait_send())
        pl.when(y_sends[way])(lambda way=way: y_copy(way).wait_send())
    wait_rows(part, members - 1, r_send.at[0])

    @pl.when(holder)
    def _():
        wait_rows(zsum, HOLDERS * lines - 1, r_send.at[1])

    @pl.when(jnp.logical_not(holder))
    def _():
        wait_rows(zsum, HOLDERS * lines, r_send.at[1])

    for level in range(HOLDERS):
        @pl.when(z == level)
        def _():
            wait_rows(zsum, len(clients[level]), r_send.at[3])

    wait_rows(total, members - 1, r_send.at[2])


def finish(
    row_count,
    total_hbm, data_hbm, ortho_hbm, coeff_hbm, upper_hbm,
    total, data, full, weights, result, coeff, upper, spread, lines, i_sems, o_sems,
):
    total_in = pltpu.make_async_copy(total_hbm, total, i_sems.at[0])
    total_in.start()
    data_in = pltpu.make_async_copy(data_hbm, data, i_sems.at[1])
    data_in.start()
    own = pl.multiple_of(lax.axis_index("basis") * 16, 16)

    total_in.wait()
    moments = unpack_full(total, 1.0 / row_count)
    lane64 = iota((64, 128), 1)
    first = jnp.where(lane64 < 16, pltpu.roll(moments[0:64], 64, 1), 0.0)
    gram_basis = jnp.where(lane64 < 64, moments[0:64], 0.0)
    zeros64 = jnp.zeros((64, 128), F32)
    both = 2.0 * first - dot_exact(gram_basis, jnp.concatenate([first, zeros64], axis=0))
    full[0:64, :] = both
    coeff[...] = full[pl.ds(own, 16), 0:16]
    coeff_out = pltpu.make_async_copy(coeff, coeff_hbm, o_sems.at[0])
    coeff_out.start()
    unit = jnp.where((iota((64, 128), 0) == lane64) & (lane64 < 16), 1.0, 0.0)
    mix = jnp.concatenate([-both, unit], axis=0)
    image = dot_exact(moments, mix)
    mix_t = mix.T[0:16]
    gram = dot_exact(mix_t, image)
    factors = factor(gram, spread, lines)
    upper[...] = jnp.where(iota((16, 16), 0) <= iota((16, 16), 1), factors[:, 0:16], 0.0)
    upper_out = pltpu.make_async_copy(upper, upper_hbm, o_sems.at[1])
    upper_out.start()
    inverse = pltpu.roll(factors, 112, 1)
    inverse = jnp.where(iota((16, 128), 1) < 16, inverse, 0.0)
    weight = dot_exact(
        inverse, jnp.concatenate([mix_t, jnp.zeros((112, 128), F32)], axis=0)
    )
    high = weight.astype(BF16).astype(F32)
    stacked = jnp.concatenate([high, weight - high], axis=0)
    weights[:, 0:80] = stacked[:, 0:80]
    weights[:, 80:160] = stacked[:, 0:80]
    data_in.wait()
    left = weights[:, 0:160].astype(BF16)
    out = result.reshape(384, 128)
    ortho_out = []
    for c in range(3):
        for t in range(8 * c, 8 * c + 8, 2):
            piece = jnp.dot(
                left, data[:, t * 128 : t * 128 + 256], preferred_element_type=F32
            )
            piece = piece[0:16] + piece[16:32]
            out[pl.ds(t, 16, stride=24), :] = piece[:, 0:128]
            out[pl.ds(t + 1, 16, stride=24), :] = piece[:, 128:256]
        ortho_out.append(
            pltpu.make_async_copy(result.at[:, c], ortho_hbm.at[:, c, 0], o_sems.at[2 + c])
        )
        ortho_out[c].start()
    coeff_out.wait()
    upper_out.wait()
    for copy in ortho_out:
        copy.wait()


def shards(space, sides, x_block, basis, material, k0, diag, ke, mass, velocities, shifts, sample):
    plane = PLANE
    share = 32 // (sides * 2)
    depth = space // plane
    row_count = 3.0 * space * x_block.shape[3] * sides * x_block.shape[4]
    vmem, smem, dma = pltpu.VMEM, pltpu.SMEM, pltpu.SemaphoreType.DMA
    block = (16, 3, 8, 128)
    scratch = [
        smem((3, 3, 8, 7), F32), smem((3, 3, 8, 7), F32), smem((3, 8), F32), smem((3, 8), F32),
        smem((8, 128), F32), smem((8, 128), F32),
        vmem((1, 8, 128), jnp.int32), vmem(block, F32), vmem((2,) + block, F32),
        vmem((2, 16, 3, 1, 128), F32), vmem((16, 3, 32, 128), F32), vmem((sides,) + block, F32), vmem(block, F32),
        vmem((63, 8, 128), F32), vmem((160, 3072), BF16), vmem((80, 128), F32),
        vmem((32, 128), F32), vmem((32, 128), F32), vmem((share, 128), F32),
        vmem((depth * plane // 2 * share, 128), F32), vmem((share, 128), F32),
        dma((10,)), dma((3, 3)), dma((3, 3)), dma((2,)), dma((2,)), dma((2,)), dma((2,)),
        dma((4,)), dma((4,)), dma((2,)),
        pltpu.SemaphoreType.REGULAR,
    ]
    whole = pl.BlockSpec(memory_space=pltpu.HBM)
    outs = pl.pallas_call(
        functools.partial(kernel, (space, sides, plane, row_count)),
        out_shape=(
            jax.ShapeDtypeStruct((32, 128), F32),
            jax.ShapeDtypeStruct((160, 3072), BF16),
        ),
        in_specs=[whole] * 9 + [pl.BlockSpec(memory_space=smem)],
        out_specs=(whole,) * 2,
        scratch_shapes=scratch,
        compiler_params=pltpu.CompilerParams(
            collective_id=0, has_side_effects=True, vmem_limit_bytes=64 * 1024 * 1024
        ),
    )(
        x_block, basis, material,
        jnp.transpose(k0, (2, 3, 0, 1)), jnp.transpose(ke, (2, 3, 0, 1)),
        diag.T, mass.T, velocities.reshape(8, 128), shifts.reshape(8, 128), sample,
    )
    return pl.pallas_call(
        functools.partial(finish, row_count),
        out_shape=(
            jax.ShapeDtypeStruct(x_block.shape, F32),
            jax.ShapeDtypeStruct((16, 16), F32),
            jax.ShapeDtypeStruct((16, 16), F32),
        ),
        in_specs=[whole] * 2,
        out_specs=(whole,) * 3,
        scratch_shapes=[
            vmem((32, 128), F32), vmem((160, 3072), BF16), vmem((80, 128), F32),
            vmem((32, 256), F32), vmem(block, F32), vmem((16, 16), F32), vmem((16, 16), F32),
            vmem((256, 128), F32), vmem((16, 128), F32), dma((2,)), dma((5,)),
        ],
        compiler_params=pltpu.CompilerParams(vmem_limit_bytes=64 * 1024 * 1024),
    )(*outs)


def solution(mesh):
    in_specs = (
        P(None, None, "space", "basis", None), P("basis", None, "space", None, None),
        P("space", "basis", None), P(), P(), P(), P(), P(), P(), P(),
    )
    out_specs = (P(None, None, "space", "basis", None), P("basis", None), P())
    body = functools.partial(shards, mesh.shape["space"], mesh.shape["basis"])
    return jax.shard_map(body, mesh=mesh, in_specs=in_specs, out_specs=out_specs, check_vma=False)
```

```python
import functools

import jax
import jax.numpy as jnp
from jax import lax
from jax.experimental import pallas as pl
from jax.experimental.pallas import tpu as pltpu
from jax.sharding import PartitionSpec as P

MESH = pl.DeviceIdType.MESH
PLANE = 8
HOLDERS = 4
EXACT = lax.Precision.HIGHEST
F32 = jnp.float32
BF16 = jnp.bfloat16


def dot_exact(a, b):
    return lax.dot_general(
        a, b, (((1,), (0,)), ((), ())), precision=EXACT, preferred_element_type=F32
    )


def iota(shape, axis):
    return lax.broadcasted_iota(jnp.int32, shape, axis)


def pick(bits, values):
    level = list(values)
    for bit in bits:
        level = [jnp.where(bit, level[i + 1], level[i]) for i in range(0, len(level), 2)]
    return level[0]


def fill_fields(mat_ref, k0, ke, diag, mass, velocities, shifts, sample, fields):
    index = sample[0]
    velocity = velocities[index // 128, index % 128]
    shift = shifts[index // 128, index % 128]
    square = velocity * velocity
    cells = mat_ref[0]
    bits = [((cells >> b) & 1) == 1 for b in range(3)]

    def offset_body(o, carry):
        for i in range(3):
            for j in range(3):
                values = [k0[i, j, m, o] - square * ke[i, j, m, o] for m in range(8)]
                fields[o * 9 + i * 3 + j] = pick(bits, values)
        return carry

    lax.fori_loop(0, 7, offset_body, 0)
    for i in range(3):
        values = [diag[i, m] - shift * mass[i, m] for m in range(8)]
        fields[4 * i] = fields[4 * i] + pick(bits, values)


def apply_stencil(xs, xh, yh, fields, applied):
    row = iota((8, 128), 0)
    lane = iota((8, 128), 1)

    def column(n, carry):
        sums = [None] * 3
        for j in range(3):
            centre = xs[n, j]
            low_y = jnp.where(
                row == 0, jnp.broadcast_to(yh[0, n, j], (8, 128)), pltpu.roll(centre, 1, 0)
            )
            high_y = jnp.where(
                row == 7, jnp.broadcast_to(yh[1, n, j], (8, 128)), pltpu.roll(centre, 7, 0)
            )
            low_z = jnp.where(lane == 0, 0.0, pltpu.roll(centre, 1, 1))
            high_z = jnp.where(lane == 127, 0.0, pltpu.roll(centre, 127, 1))
            views = [centre, xh[0, n, j], xh[1, n, j], low_y, high_y, low_z, high_z]
            for o in range(7):
                for i in range(3):
                    term = fields[o * 9 + i * 3 + j] * views[o]
                    sums[i] = term if sums[i] is None else sums[i] + term
        for i in range(3):
            applied[n, i] = sums[i]
        return carry

    lax.fori_loop(0, 16, column, 0)


def split_rows(raw, data, first, part):
    def tile(i, carry):
        t = part * 8 + i
        block = raw[pl.ds(t, 16, stride=24), :]
        high = block.astype(BF16)
        rest = (block - high.astype(F32)).astype(BF16)
        lanes = pl.ds(pl.multiple_of(t * 128, 128), 128)
        data[pl.ds(first, 16), lanes] = high
        data[pl.ds(80 + first, 16), lanes] = rest
        return carry

    lax.fori_loop(0, 8, tile, 0, unroll=True)


def pack_upper(full, packed):
    lane = iota((16, 128), 1)
    rows = [full[16 * g : 16 * g + 16, :] for g in range(5)]
    packed[0:16, :] = jnp.where(lane < 80, rows[0], pltpu.roll(rows[2], 48, 1))
    packed[16:32, :] = jnp.where(
        lane < 64,
        pltpu.roll(rows[1], 112, 1),
        jnp.where(
            lane < 96,
            pltpu.roll(rows[3], 16, 1),
            jnp.where(lane < 112, pltpu.roll(rows[4], 32, 1), 0.0),
        ),
    )


def unpack_full(packed, scale):
    lane = iota((16, 128), 1)
    one, two = packed[0:16, :], packed[16:32, :]
    parts = [
        one,
        pltpu.roll(two, 16, 1),
        pltpu.roll(one, 80, 1),
        pltpu.roll(two, 112, 1),
        pltpu.roll(two, 96, 1),
    ]
    rows = []
    for g in range(5):
        weight = jnp.where(lane < 16 * g + 16, 0.5 * scale, scale)
        rows.append(jnp.where((lane >= 16 * g) & (lane < 80), parts[g] * weight, 0.0))
    rows.append(jnp.zeros((48, 128), F32))
    upper = jnp.concatenate(rows, axis=0)
    return upper + upper.T


def factor(gram, spread, lines):
    lane = iota((8, 128), 1)
    for j in range(16):
        spread[16 * j : 16 * j + 16, :] = jnp.broadcast_to(gram[:, j : j + 1], (16, 128))
    lines[...] = gram

    def full(ref, r):
        return jnp.broadcast_to(ref[r : r + 1, :], (8, 128))

    entry = {(i, j): full(spread, 16 * j + i) for j in range(16) for i in range(j, 16)}
    rows = [
        jnp.where(lane < 16, full(lines, i), jnp.where(lane == 16 + i, 1.0, 0.0))
        for i in range(16)
    ]
    for k in range(16):
        pivot = entry[k, k]
        inverse = 1.0 / pivot
        for i in range(k + 1, 16):
            scale = entry[i, k] * inverse
            for j in range(k + 1, i + 1):
                entry[i, j] = entry[i, j] - scale * entry[j, k]
            rows[i] = rows[i] - scale * rows[k]
        root = lax.rsqrt(pivot)
        root = root * (1.5 - 0.5 * pivot * root * root)
        lines[k : k + 1, :] = (rows[k] * root)[0:1]
    return lines[...]


def kernel(
    sizes,
    x_hbm, basis_hbm, mat_hbm, k0_hbm, ke_hbm, diag_hbm, mass_hbm, vel_hbm, shift_hbm, sample,
    total, data_hbm,
    k0, ke, diag, mass, velocities, shifts,
    mat, xs, xh, yh, whole, raw, applied, fields, data, full, packed, part, zpart, zsum, total_z,
    local_sems, b_send, b_recv, x_send, x_recv, y_send, y_recv, r_send, r_recv, o_sems, ready,
):
    space, sides, plane, row_count = sizes
    depth = space // plane
    lines = plane // 2
    members = sides * 2
    share = 32 // members
    s = lax.axis_index("space")
    b = lax.axis_index("basis")
    z = s // plane
    spot = s - z * plane
    x = spot // 2
    core = spot - 2 * x
    me = b * 2 + core
    place = z * lines + x
    holder = z < HOLDERS
    turn = (depth + HOLDERS) // 2
    served = jnp.where(z < turn, HOLDERS - 1, 0)
    clients = {0: range(turn, depth), HOLDERS - 1: range(HOLDERS, turn)}

    def members_each(act):
        sites = sorted(range(sides), key=lambda d: -min(d, sides - d))
        for dy in sites:
            side = lax.rem(b + dy, sides)
            for other in ((1 - core, core) if dy else (1 - core,)):
                act(side * 2 + other, (z * plane + x * 2 + other, side))

    def spot_at(level, column):
        return level * plane + column * 2 + core, b

    def holders_each(act):
        for level in range(HOLDERS):
            for column in range(lines):
                pl.when(place != level * lines + column)(
                    lambda level=level, column=column: act(spot_at(level, column))
                )

    barrier = pltpu.get_barrier_semaphore()

    def greet(peer):
        pl.semaphore_signal(barrier, inc=1, device_id=peer, device_id_type=MESH)

    beside = s + 2 * core - 1
    has_beside = (beside >= 0) & (beside < space)
    @pl.when(has_beside)
    def _():
        greet((beside, b))

    members_each(lambda index, peer: greet(peer))

    @pl.when(holder)
    def _():
        for level in range(HOLDERS):
            for column in range(lines):
                pl.when(place != level * lines + column)(
                    lambda level=level, column=column: greet(spot_at(level, column))
                )

        @pl.loop(HOLDERS, depth)
        def _(level):
            for column in range(lines):
                greet(spot_at(level, column))

    small = [
        (vel_hbm, velocities), (shift_hbm, shifts), (k0_hbm, k0),
        (ke_hbm, ke), (diag_hbm, diag), (mass_hbm, mass), (mat_hbm, mat),
        (basis_hbm.at[:, :, 0], whole), (x_hbm.at[:, :, 0], xs),
        (basis_hbm.at[:, :, 0, pl.ds(pl.multiple_of(b * 8, 8), 8), :], raw.at[b]),
    ]
    small = [
        pltpu.make_async_copy(source, target, local_sems.at[i])
        for i, (source, target) in enumerate(small)
    ]
    for copy in small:
        copy.start()

    known = members - 1 + HOLDERS * lines
    known = known + jnp.where(has_beside, 1, 0) - jnp.where(holder, 1, 0)
    pl.semaphore_wait(barrier, known)

    @pl.when(jnp.logical_not(holder))
    def _():
        pl.semaphore_signal(
            ready, inc=1, device_id=spot_at(served, x), device_id_type=MESH
        )

    def remote(source, target, send, recv, peer):
        return pltpu.make_async_remote_copy(
            src_ref=source, dst_ref=target, send_sem=send, recv_sem=recv,
            device_id=peer, device_id_type=MESH,
        )

    def basis_copy(k, c):
        side = lax.rem(b + k, sides)
        return remote(
            whole.at[:, c, pl.ds(pl.multiple_of(side * 8, 8), 8), :],
            raw.at[b, :, c], b_send.at[k - 1, c], b_recv.at[k - 1, c], (s, side),
        )

    def x_copy(way):
        peer = s + 1 if way == 0 else s - 1
        return remote(x_hbm.at[:, :, 0], xh.at[way], x_send.at[way], x_recv.at[way], (peer, b))

    def y_copy(way):
        peer = b + 1 if way == 0 else b - 1
        edge = 7 if way == 0 else 0
        return remote(
            x_hbm.at[:, :, 0, edge : edge + 1, :], yh.at[way], y_send.at[way], y_recv.at[way],
            (s, peer),
        )

    x_sends = [s < space - 1, s > 0]
    x_gets = [s > 0, s < space - 1]
    y_sends = [b < sides - 1, b > 0]
    y_gets = [b > 0, b < sides - 1]
    for way in range(2):
        pl.when(y_sends[way])(lambda way=way: y_copy(way).start())
    small[7].wait()
    for c in range(3):
        for k in (2, 1, 3):
            basis_copy(k, c).start()
    for way in range(2):
        pl.when(x_sends[way])(lambda way=way: x_copy(way).start())

    for copy in small[:7]:
        copy.wait()
    fill_fields(mat, k0, ke, diag, mass, velocities, shifts, sample, fields)
    small[9].wait()
    own = pl.multiple_of(b * 16, 16)
    for c in range(3):
        split_rows(raw.at[b].reshape(384, 128), data, own, c)
    small[8].wait()

    for way in range(2):
        @pl.when(jnp.logical_not(x_gets[way]))
        def _():
            xh[way] = jnp.zeros(xs.shape, F32)

        @pl.when(jnp.logical_not(y_gets[way]))
        def _():
            yh[way] = jnp.zeros((16, 3, 1, 128), F32)

        pl.when(x_gets[way])(lambda way=way: x_copy(way).wait_recv())
        pl.when(y_gets[way])(lambda way=way: y_copy(way).wait_recv())

    apply_stencil(xs, xh, yh, fields, applied)
    for c in range(3):
        split_rows(applied.reshape(384, 128), data, 64, c)

    products = None
    for c in range(3):
        for k in (1, 3, 2):
            basis_copy(k, c).wait_recv()
            side = lax.rem(b + sides - k, sides)
            split_rows(raw.at[side].reshape(384, 128), data, pl.multiple_of(side * 16, 16), c)
        piece = data[:, c * 1024 : (c + 1) * 1024]
        term = lax.dot_general(
            piece, piece, (((1,), (1,)), ((), ())), preferred_element_type=F32
        )
        products = term if products is None else products + term
    products = products[0:80] + products[80:160]
    full[:, 0:80] = products[:, 0:80] + products[:, 80:160]
    pack_upper(full, packed)

    def rows_of(index):
        return pl.ds(index * share, share)

    def scatter(index, peer):
        remote(
            packed.at[rows_of(index)], part.at[rows_of(me)], r_send.at[0], r_recv.at[0], peer
        ).start()

    def to_holder(peer):
        remote(zpart, zsum.at[rows_of(place)], r_send.at[1], r_recv.at[1], peer).start()

    def to_client(level):
        remote(total_z, total_z, r_send.at[3], r_recv.at[3], spot_at(level, x)).start()

    def gather(index, peer):
        remote(total_z, total.at[rows_of(me)], r_send.at[2], r_recv.at[2], peer).start()

    def fold(ref, count):
        tiles = [ref[8 * i : 8 * i + 8] for i in range(count * share // 8)]
        while len(tiles) > 1:
            half = (len(tiles) + 1) // 2
            tiles = [
                tiles[i] + tiles[i + half] if i + half < len(tiles) else tiles[i]
                for i in range(half)
            ]
        return tiles[0][0:4] + tiles[0][4:8]

    def wait_rows(ref, count, sem):
        view = ref.at[pl.ds(0, count * share)]
        pltpu.make_async_copy(view, view, sem).wait()

    members_each(scatter)
    part[rows_of(me)] = packed[rows_of(me)]
    data_out = pltpu.make_async_copy(data, data_hbm, o_sems.at[0])
    data_out.start()
    wait_rows(part, members - 1, r_recv.at[0])
    zpart[...] = fold(part, members)
    holders_each(to_holder)

    @pl.when(holder)
    def _():
        zsum[rows_of(place)] = zpart[...]
        wait_rows(zsum, depth * lines - 1, r_recv.at[1])
        total_z[...] = fold(zsum, depth * lines)
        members_each(gather)

    for level in clients:
        @pl.when(z == level)
        def _():
            pl.semaphore_wait(ready, len(clients[level]))
            for client in clients[level]:
                to_client(client)

    @pl.when(jnp.logical_not(holder))
    def _():
        wait_rows(total_z, 1, r_recv.at[3])
        members_each(gather)

    own_rows = pltpu.make_async_copy(total_z, total.at[rows_of(me)], o_sems.at[1])
    own_rows.start()
    data_out.wait()
    for c in range(3):
        for k in (1, 2, 3):
            basis_copy(k, c).wait_send()
    for way in range(2):
        pl.when(x_sends[way])(lambda way=way: x_copy(way).wait_send())
        pl.when(y_sends[way])(lambda way=way: y_copy(way).wait_send())
    wait_rows(part, members - 1, r_send.at[0])

    @pl.when(holder)
    def _():
        wait_rows(zsum, HOLDERS * lines - 1, r_send.at[1])

    @pl.when(jnp.logical_not(holder))
    def _():
        wait_rows(zsum, HOLDERS * lines, r_send.at[1])

    for level in clients:
        @pl.when(z == level)
        def _():
            wait_rows(zsum, len(clients[level]), r_send.at[3])

    wait_rows(total, members - 1, r_recv.at[2])
    own_rows.wait()
    wait_rows(total, members - 1, r_send.at[2])


def finish(
    row_count,
    total_hbm, data_hbm, ortho_hbm, coeff_hbm, upper_hbm,
    total, data, full, weights, result, coeff, upper, spread, lines, i_sems, o_sems,
):
    total_in = pltpu.make_async_copy(total_hbm, total, i_sems.at[0])
    total_in.start()
    data_in = pltpu.make_async_copy(data_hbm, data, i_sems.at[1])
    data_in.start()
    own = pl.multiple_of(lax.axis_index("basis") * 16, 16)

    total_in.wait()
    moments = unpack_full(total, 1.0 / row_count)
    lane64 = iota((64, 128), 1)
    first = jnp.where(lane64 < 16, pltpu.roll(moments[0:64], 64, 1), 0.0)
    gram_basis = jnp.where(lane64 < 64, moments[0:64], 0.0)
    zeros64 = jnp.zeros((64, 128), F32)
    both = 2.0 * first - dot_exact(gram_basis, jnp.concatenate([first, zeros64], axis=0))
    full[0:64, :] = both
    coeff[...] = full[pl.ds(own, 16), 0:16]
    coeff_out = pltpu.make_async_copy(coeff, coeff_hbm, o_sems.at[0])
    coeff_out.start()
    unit = jnp.where((iota((64, 128), 0) == lane64) & (lane64 < 16), 1.0, 0.0)
    mix = jnp.concatenate([-both, unit], axis=0)
    image = dot_exact(moments, mix)
    mix_t = mix.T[0:16]
    gram = dot_exact(mix_t, image)
    factors = factor(gram, spread, lines)
    upper[...] = jnp.where(iota((16, 16), 0) <= iota((16, 16), 1), factors[:, 0:16], 0.0)
    upper_out = pltpu.make_async_copy(upper, upper_hbm, o_sems.at[1])
    upper_out.start()
    inverse = pltpu.roll(factors, 112, 1)
    inverse = jnp.where(iota((16, 128), 1) < 16, inverse, 0.0)
    weight = dot_exact(
        inverse, jnp.concatenate([mix_t, jnp.zeros((112, 128), F32)], axis=0)
    )
    high = weight.astype(BF16).astype(F32)
    stacked = jnp.concatenate([high, weight - high], axis=0)
    weights[:, 0:80] = stacked[:, 0:80]
    weights[:, 80:160] = stacked[:, 0:80]
    data_in.wait()
    left = weights[:, 0:160].astype(BF16)
    out = result.reshape(384, 128)
    ortho_out = []
    for c in range(3):
        for t in range(8 * c, 8 * c + 8, 2):
            piece = jnp.dot(
                left, data[:, t * 128 : t * 128 + 256], preferred_element_type=F32
            )
            piece = piece[0:16] + piece[16:32]
            out[pl.ds(t, 16, stride=24), :] = piece[:, 0:128]
            out[pl.ds(t + 1, 16, stride=24), :] = piece[:, 128:256]
        ortho_out.append(
            pltpu.make_async_copy(result.at[:, c], ortho_hbm.at[:, c, 0], o_sems.at[2 + c])
        )
        ortho_out[c].start()
    coeff_out.wait()
    upper_out.wait()
    for copy in ortho_out:
        copy.wait()


def shards(space, sides, x_block, basis, material, k0, diag, ke, mass, velocities, shifts, sample):
    plane = PLANE
    share = 32 // (sides * 2)
    depth = space // plane
    row_count = 3.0 * space * x_block.shape[3] * sides * x_block.shape[4]
    vmem, smem, dma = pltpu.VMEM, pltpu.SMEM, pltpu.SemaphoreType.DMA
    block = (16, 3, 8, 128)
    scratch = [
        smem((3, 3, 8, 7), F32), smem((3, 3, 8, 7), F32), smem((3, 8), F32), smem((3, 8), F32),
        smem((8, 128), F32), smem((8, 128), F32),
        vmem((1, 8, 128), jnp.int32), vmem(block, F32), vmem((2,) + block, F32),
        vmem((2, 16, 3, 1, 128), F32), vmem((16, 3, 32, 128), F32), vmem((sides,) + block, F32), vmem(block, F32),
        vmem((63, 8, 128), F32), vmem((160, 3072), BF16), vmem((80, 128), F32),
        vmem((32, 128), F32), vmem((32, 128), F32), vmem((share, 128), F32),
        vmem((depth * plane // 2 * share, 128), F32), vmem((share, 128), F32),
        dma((10,)), dma((3, 3)), dma((3, 3)), dma((2,)), dma((2,)), dma((2,)), dma((2,)),
        dma((4,)), dma((4,)), dma((2,)),
        pltpu.SemaphoreType.REGULAR,
    ]
    whole = pl.BlockSpec(memory_space=pltpu.HBM)
    outs = pl.pallas_call(
        functools.partial(kernel, (space, sides, plane, row_count)),
        out_shape=(
            jax.ShapeDtypeStruct((32, 128), F32),
            jax.ShapeDtypeStruct((160, 3072), BF16),
        ),
        in_specs=[whole] * 9 + [pl.BlockSpec(memory_space=smem)],
        out_specs=(whole,) * 2,
        scratch_shapes=scratch,
        compiler_params=pltpu.CompilerParams(
            collective_id=0, has_side_effects=True, vmem_limit_bytes=64 * 1024 * 1024
        ),
    )(
        x_block, basis, material,
        jnp.transpose(k0, (2, 3, 0, 1)), jnp.transpose(ke, (2, 3, 0, 1)),
        diag.T, mass.T, velocities.reshape(8, 128), shifts.reshape(8, 128), sample,
    )
    return pl.pallas_call(
        functools.partial(finish, row_count),
        out_shape=(
            jax.ShapeDtypeStruct(x_block.shape, F32),
            jax.ShapeDtypeStruct((16, 16), F32),
            jax.ShapeDtypeStruct((16, 16), F32),
        ),
        in_specs=[whole] * 2,
        out_specs=(whole,) * 3,
        scratch_shapes=[
            vmem((32, 128), F32), vmem((160, 3072), BF16), vmem((80, 128), F32),
            vmem((32, 256), F32), vmem(block, F32), vmem((16, 16), F32), vmem((16, 16), F32),
            vmem((256, 128), F32), vmem((16, 128), F32), dma((2,)), dma((5,)),
        ],
        compiler_params=pltpu.CompilerParams(vmem_limit_bytes=64 * 1024 * 1024),
    )(*outs)


def solution(mesh):
    in_specs = (
        P(None, None, "space", "basis", None), P("basis", None, "space", None, None),
        P("space", "basis", None), P(), P(), P(), P(), P(), P(), P(),
    )
    out_specs = (P(None, None, "space", "basis", None), P("basis", None), P())
    body = functools.partial(shards, mesh.shape["space"], mesh.shape["basis"])
    return jax.shard_map(body, mesh=mesh, in_specs=in_specs, out_specs=out_specs, check_vma=False)
```

```python
import functools

import jax
import jax.numpy as jnp
from jax import lax
from jax.experimental import pallas as pl
from jax.experimental.pallas import tpu as pltpu
from jax.sharding import PartitionSpec as P

MESH = pl.DeviceIdType.MESH
PLANE = 8
HOLDERS = 4
EXACT = lax.Precision.HIGHEST
F32 = jnp.float32
BF16 = jnp.bfloat16


def dot_exact(a, b):
    return lax.dot_general(
        a, b, (((1,), (0,)), ((), ())), precision=EXACT, preferred_element_type=F32
    )


def iota(shape, axis):
    return lax.broadcasted_iota(jnp.int32, shape, axis)


def pick(bits, values):
    level = list(values)
    for bit in bits:
        level = [jnp.where(bit, level[i + 1], level[i]) for i in range(0, len(level), 2)]
    return level[0]


def fill_fields(mat_ref, k0, ke, diag, mass, velocities, shifts, sample, fields):
    index = sample[0]
    velocity = velocities[index // 128, index % 128]
    shift = shifts[index // 128, index % 128]
    square = velocity * velocity
    cells = mat_ref[0]
    bits = [((cells >> b) & 1) == 1 for b in range(3)]

    def offset_body(o, carry):
        for i in range(3):
            for j in range(3):
                values = [k0[i, j, m, o] - square * ke[i, j, m, o] for m in range(8)]
                fields[o * 9 + i * 3 + j] = pick(bits, values)
        return carry

    lax.fori_loop(0, 7, offset_body, 0)
    for i in range(3):
        values = [diag[i, m] - shift * mass[i, m] for m in range(8)]
        fields[4 * i] = fields[4 * i] + pick(bits, values)


def apply_stencil(xs, xh, yh, fields, applied):
    row = iota((8, 128), 0)
    lane = iota((8, 128), 1)

    def column(n, carry):
        sums = [None] * 3
        for j in range(3):
            centre = xs[n, j]
            low_y = jnp.where(
                row == 0, jnp.broadcast_to(yh[0, n, j], (8, 128)), pltpu.roll(centre, 1, 0)
            )
            high_y = jnp.where(
                row == 7, jnp.broadcast_to(yh[1, n, j], (8, 128)), pltpu.roll(centre, 7, 0)
            )
            low_z = jnp.where(lane == 0, 0.0, pltpu.roll(centre, 1, 1))
            high_z = jnp.where(lane == 127, 0.0, pltpu.roll(centre, 127, 1))
            views = [centre, xh[0, n, j], xh[1, n, j], low_y, high_y, low_z, high_z]
            for o in range(7):
                for i in range(3):
                    term = fields[o * 9 + i * 3 + j] * views[o]
                    sums[i] = term if sums[i] is None else sums[i] + term
        for i in range(3):
            applied[n, i] = sums[i]
        return carry

    lax.fori_loop(0, 16, column, 0)


def split_rows(raw, data, first, part):
    def tile(i, carry):
        t = part * 8 + i
        block = raw[pl.ds(t, 16, stride=24), :]
        high = block.astype(BF16)
        rest = (block - high.astype(F32)).astype(BF16)
        lanes = pl.ds(pl.multiple_of(t * 128, 128), 128)
        data[pl.ds(first, 16), lanes] = high
        data[pl.ds(80 + first, 16), lanes] = rest
        return carry

    lax.fori_loop(0, 8, tile, 0, unroll=True)


def pack_upper(full, packed):
    lane = iota((16, 128), 1)
    rows = [full[16 * g : 16 * g + 16, :] for g in range(5)]
    packed[0:16, :] = jnp.where(lane < 80, rows[0], pltpu.roll(rows[2], 48, 1))
    packed[16:32, :] = jnp.where(
        lane < 64,
        pltpu.roll(rows[1], 112, 1),
        jnp.where(
            lane < 96,
            pltpu.roll(rows[3], 16, 1),
            jnp.where(lane < 112, pltpu.roll(rows[4], 32, 1), 0.0),
        ),
    )


def unpack_full(packed, scale):
    lane = iota((16, 128), 1)
    one, two = packed[0:16, :], packed[16:32, :]
    parts = [
        one,
        pltpu.roll(two, 16, 1),
        pltpu.roll(one, 80, 1),
        pltpu.roll(two, 112, 1),
        pltpu.roll(two, 96, 1),
    ]
    rows = []
    for g in range(5):
        weight = jnp.where(lane < 16 * g + 16, 0.5 * scale, scale)
        rows.append(jnp.where((lane >= 16 * g) & (lane < 80), parts[g] * weight, 0.0))
    rows.append(jnp.zeros((48, 128), F32))
    upper = jnp.concatenate(rows, axis=0)
    return upper + upper.T


def factor(gram, spread, lines):
    lane = iota((8, 128), 1)
    for j in range(16):
        spread[16 * j : 16 * j + 16, :] = jnp.broadcast_to(gram[:, j : j + 1], (16, 128))
    lines[...] = gram

    def full(ref, r):
        return jnp.broadcast_to(ref[r : r + 1, :], (8, 128))

    entry = {(i, j): full(spread, 16 * j + i) for j in range(16) for i in range(j, 16)}
    rows = [
        jnp.where(lane < 16, full(lines, i), jnp.where(lane == 16 + i, 1.0, 0.0))
        for i in range(16)
    ]
    for k in range(16):
        pivot = entry[k, k]
        inverse = 1.0 / pivot
        for i in range(k + 1, 16):
            scale = entry[i, k] * inverse
            for j in range(k + 1, i + 1):
                entry[i, j] = entry[i, j] - scale * entry[j, k]
            rows[i] = rows[i] - scale * rows[k]
        root = lax.rsqrt(pivot)
        root = root * (1.5 - 0.5 * pivot * root * root)
        lines[k : k + 1, :] = (rows[k] * root)[0:1]
    return lines[...]


def kernel(
    sizes,
    x_hbm, basis_hbm, mat_hbm, k0_hbm, ke_hbm, diag_hbm, mass_hbm, vel_hbm, shift_hbm, sample,
    total, data_hbm,
    k0, ke, diag, mass, velocities, shifts,
    mat, xs, xh, yh, whole, raw, applied, fields, data, full, packed, part, zpart, zsum, total_z,
    local_sems, b_send, b_recv, x_send, x_recv, y_send, y_recv, r_send, r_recv, o_sems, ready,
):
    space, sides, plane, row_count = sizes
    depth = space // plane
    lines = plane // 2
    members = sides * 2
    share = 32 // members
    s = lax.axis_index("space")
    b = lax.axis_index("basis")
    z = s // plane
    spot = s - z * plane
    x = spot // 2
    core = spot - 2 * x
    me = b * 2 + core
    place = z * lines + x
    holder = z < HOLDERS
    turn = (depth + HOLDERS) // 2
    served = jnp.where(z < turn, HOLDERS - 1, 0)
    clients = {0: range(turn, depth), HOLDERS - 1: range(HOLDERS, turn)}

    def members_each(act):
        sites = sorted(range(sides), key=lambda d: -min(d, sides - d))
        for dy in sites:
            side = lax.rem(b + dy, sides)
            for other in ((1 - core, core) if dy else (1 - core,)):
                act(side * 2 + other, (z * plane + x * 2 + other, side))

    def spot_at(level, column):
        return level * plane + column * 2 + core, b

    def holders_each(act):
        for level in range(HOLDERS):
            for column in range(lines):
                pl.when(place != level * lines + column)(
                    lambda level=level, column=column: act(spot_at(level, column))
                )

    barrier = pltpu.get_barrier_semaphore()

    def greet(peer):
        pl.semaphore_signal(barrier, inc=1, device_id=peer, device_id_type=MESH)

    beside = s + 2 * core - 1
    has_beside = (beside >= 0) & (beside < space)
    @pl.when(has_beside)
    def _():
        greet((beside, b))

    members_each(lambda index, peer: greet(peer))

    @pl.when(holder)
    def _():
        for level in range(HOLDERS):
            for column in range(lines):
                pl.when(place != level * lines + column)(
                    lambda level=level, column=column: greet(spot_at(level, column))
                )

        @pl.loop(HOLDERS, depth)
        def _(level):
            for column in range(lines):
                greet(spot_at(level, column))

    small = [
        (vel_hbm, velocities), (shift_hbm, shifts), (k0_hbm, k0),
        (ke_hbm, ke), (diag_hbm, diag), (mass_hbm, mass), (mat_hbm, mat),
        (basis_hbm.at[:, :, 0], whole), (x_hbm.at[:, :, 0], xs),
        (basis_hbm.at[:, :, 0, pl.ds(pl.multiple_of(b * 8, 8), 8), :], raw.at[b]),
    ]
    small = [
        pltpu.make_async_copy(source, target, local_sems.at[i])
        for i, (source, target) in enumerate(small)
    ]
    for copy in small:
        copy.start()

    known = members - 1 + HOLDERS * lines
    known = known + jnp.where(has_beside, 1, 0) - jnp.where(holder, 1, 0)
    pl.semaphore_wait(barrier, known)

    @pl.when(jnp.logical_not(holder))
    def _():
        pl.semaphore_signal(
            ready, inc=1, device_id=spot_at(served, x), device_id_type=MESH
        )

    def remote(source, target, send, recv, peer):
        return pltpu.make_async_remote_copy(
            src_ref=source, dst_ref=target, send_sem=send, recv_sem=recv,
            device_id=peer, device_id_type=MESH,
        )

    def basis_copy(k, c):
        side = lax.rem(b + k, sides)
        return remote(
            whole.at[:, c, pl.ds(pl.multiple_of(side * 8, 8), 8), :],
            raw.at[b, :, c], b_send.at[k - 1, c], b_recv.at[k - 1, c], (s, side),
        )

    def x_copy(way):
        peer = s + 1 if way == 0 else s - 1
        return remote(x_hbm.at[:, :, 0], xh.at[way], x_send.at[way], x_recv.at[way], (peer, b))

    def y_copy(way):
        peer = b + 1 if way == 0 else b - 1
        edge = 7 if way == 0 else 0
        return remote(
            x_hbm.at[:, :, 0, edge : edge + 1, :], yh.at[way], y_send.at[way], y_recv.at[way],
            (s, peer),
        )

    x_sends = [s < space - 1, s > 0]
    x_gets = [s > 0, s < space - 1]
    y_sends = [b < sides - 1, b > 0]
    y_gets = [b > 0, b < sides - 1]
    small[7].wait()
    for c in range(3):
        for k in (2, 1, 3):
            basis_copy(k, c).start()
        if c == 0:
            for way in range(2):
                pl.when(y_sends[way])(lambda way=way: y_copy(way).start())
    for way in range(2):
        pl.when(x_sends[way])(lambda way=way: x_copy(way).start())

    for copy in small[:7]:
        copy.wait()
    fill_fields(mat, k0, ke, diag, mass, velocities, shifts, sample, fields)
    small[9].wait()
    own = pl.multiple_of(b * 16, 16)
    for c in range(3):
        split_rows(raw.at[b].reshape(384, 128), data, own, c)
    small[8].wait()

    for way in range(2):
        @pl.when(jnp.logical_not(x_gets[way]))
        def _():
            xh[way] = jnp.zeros(xs.shape, F32)

        @pl.when(jnp.logical_not(y_gets[way]))
        def _():
            yh[way] = jnp.zeros((16, 3, 1, 128), F32)

        pl.when(x_gets[way])(lambda way=way: x_copy(way).wait_recv())
        pl.when(y_gets[way])(lambda way=way: y_copy(way).wait_recv())

    apply_stencil(xs, xh, yh, fields, applied)
    for c in range(3):
        split_rows(applied.reshape(384, 128), data, 64, c)

    products = None
    for c in range(3):
        for k in (1, 3, 2):
            basis_copy(k, c).wait_recv()
            side = lax.rem(b + sides - k, sides)
            split_rows(raw.at[side].reshape(384, 128), data, pl.multiple_of(side * 16, 16), c)
        piece = data[:, c * 1024 : (c + 1) * 1024]
        term = lax.dot_general(
            piece, piece, (((1,), (1,)), ((), ())), preferred_element_type=F32
        )
        products = term if products is None else products + term
    products = products[0:80] + products[80:160]
    full[:, 0:80] = products[:, 0:80] + products[:, 80:160]
    pack_upper(full, packed)

    def rows_of(index):
        return pl.ds(index * share, share)

    def scatter(index, peer):
        remote(
            packed.at[rows_of(index)], part.at[rows_of(me)], r_send.at[0], r_recv.at[0], peer
        ).start()

    def to_holder(peer):
        remote(zpart, zsum.at[rows_of(place)], r_send.at[1], r_recv.at[1], peer).start()

    def to_client(level):
        remote(total_z, total_z, r_send.at[3], r_recv.at[3], spot_at(level, x)).start()

    def gather(index, peer):
        remote(total_z, total.at[rows_of(me)], r_send.at[2], r_recv.at[2], peer).start()

    def fold(ref, count):
        tiles = [ref[8 * i : 8 * i + 8] for i in range(count * share // 8)]
        while len(tiles) > 1:
            half = (len(tiles) + 1) // 2
            tiles = [
                tiles[i] + tiles[i + half] if i + half < len(tiles) else tiles[i]
                for i in range(half)
            ]
        return tiles[0][0:4] + tiles[0][4:8]

    def wait_rows(ref, count, sem):
        view = ref.at[pl.ds(0, count * share)]
        pltpu.make_async_copy(view, view, sem).wait()

    members_each(scatter)
    part[rows_of(me)] = packed[rows_of(me)]
    data_out = pltpu.make_async_copy(data, data_hbm, o_sems.at[0])
    data_out.start()
    wait_rows(part, members - 1, r_recv.at[0])
    zpart[...] = fold(part, members)
    holders_each(to_holder)

    @pl.when(holder)
    def _():
        zsum[rows_of(place)] = zpart[...]
        wait_rows(zsum, depth * lines - 1, r_recv.at[1])
        total_z[...] = fold(zsum, depth * lines)
        members_each(gather)

    for level in clients:
        @pl.when(z == level)
        def _():
            pl.semaphore_wait(ready, len(clients[level]))
            for client in clients[level]:
                to_client(client)

    @pl.when(jnp.logical_not(holder))
    def _():
        wait_rows(total_z, 1, r_recv.at[3])
        members_each(gather)

    own_rows = pltpu.make_async_copy(total_z, total.at[rows_of(me)], o_sems.at[1])
    own_rows.start()
    data_out.wait()
    for c in range(3):
        for k in (1, 2, 3):
            basis_copy(k, c).wait_send()
    for way in range(2):
        pl.when(x_sends[way])(lambda way=way: x_copy(way).wait_send())
        pl.when(y_sends[way])(lambda way=way: y_copy(way).wait_send())
    wait_rows(part, members - 1, r_send.at[0])

    @pl.when(holder)
    def _():
        wait_rows(zsum, HOLDERS * lines - 1, r_send.at[1])

    @pl.when(jnp.logical_not(holder))
    def _():
        wait_rows(zsum, HOLDERS * lines, r_send.at[1])

    for level in clients:
        @pl.when(z == level)
        def _():
            wait_rows(zsum, len(clients[level]), r_send.at[3])

    wait_rows(total, members - 1, r_recv.at[2])
    own_rows.wait()
    wait_rows(total, members - 1, r_send.at[2])


def finish(
    row_count,
    total_hbm, data_hbm, ortho_hbm, coeff_hbm, upper_hbm,
    total, data, full, weights, result, coeff, upper, spread, lines, i_sems, o_sems,
):
    total_in = pltpu.make_async_copy(total_hbm, total, i_sems.at[0])
    total_in.start()
    data_in = pltpu.make_async_copy(data_hbm, data, i_sems.at[1])
    data_in.start()
    own = pl.multiple_of(lax.axis_index("basis") * 16, 16)

    total_in.wait()
    moments = unpack_full(total, 1.0 / row_count)
    lane64 = iota((64, 128), 1)
    first = jnp.where(lane64 < 16, pltpu.roll(moments[0:64], 64, 1), 0.0)
    gram_basis = jnp.where(lane64 < 64, moments[0:64], 0.0)
    zeros64 = jnp.zeros((64, 128), F32)
    both = 2.0 * first - dot_exact(gram_basis, jnp.concatenate([first, zeros64], axis=0))
    full[0:64, :] = both
    coeff[...] = full[pl.ds(own, 16), 0:16]
    coeff_out = pltpu.make_async_copy(coeff, coeff_hbm, o_sems.at[0])
    coeff_out.start()
    unit = jnp.where((iota((64, 128), 0) == lane64) & (lane64 < 16), 1.0, 0.0)
    mix = jnp.concatenate([-both, unit], axis=0)
    image = dot_exact(moments, mix)
    mix_t = mix.T[0:16]
    gram = dot_exact(mix_t, image)
    factors = factor(gram, spread, lines)
    upper[...] = jnp.where(iota((16, 16), 0) <= iota((16, 16), 1), factors[:, 0:16], 0.0)
    upper_out = pltpu.make_async_copy(upper, upper_hbm, o_sems.at[1])
    upper_out.start()
    inverse = pltpu.roll(factors, 112, 1)
    inverse = jnp.where(iota((16, 128), 1) < 16, inverse, 0.0)
    weight = dot_exact(
        inverse, jnp.concatenate([mix_t, jnp.zeros((112, 128), F32)], axis=0)
    )
    high = weight.astype(BF16).astype(F32)
    stacked = jnp.concatenate([high, weight - high], axis=0)
    weights[:, 0:80] = stacked[:, 0:80]
    weights[:, 80:160] = stacked[:, 0:80]
    data_in.wait()
    left = weights[:, 0:160].astype(BF16)
    out = result.reshape(384, 128)
    ortho_out = []
    for c in range(3):
        for t in range(8 * c, 8 * c + 8, 2):
            piece = jnp.dot(
                left, data[:, t * 128 : t * 128 + 256], preferred_element_type=F32
            )
            piece = piece[0:16] + piece[16:32]
            out[pl.ds(t, 16, stride=24), :] = piece[:, 0:128]
            out[pl.ds(t + 1, 16, stride=24), :] = piece[:, 128:256]
        ortho_out.append(
            pltpu.make_async_copy(result.at[:, c], ortho_hbm.at[:, c, 0], o_sems.at[2 + c])
        )
        ortho_out[c].start()
    coeff_out.wait()
    upper_out.wait()
    for copy in ortho_out:
        copy.wait()


def shards(space, sides, x_block, basis, material, k0, diag, ke, mass, velocities, shifts, sample):
    plane = PLANE
    share = 32 // (sides * 2)
    depth = space // plane
    row_count = 3.0 * space * x_block.shape[3] * sides * x_block.shape[4]
    vmem, smem, dma = pltpu.VMEM, pltpu.SMEM, pltpu.SemaphoreType.DMA
    block = (16, 3, 8, 128)
    scratch = [
        smem((3, 3, 8, 7), F32), smem((3, 3, 8, 7), F32), smem((3, 8), F32), smem((3, 8), F32),
        smem((8, 128), F32), smem((8, 128), F32),
        vmem((1, 8, 128), jnp.int32), vmem(block, F32), vmem((2,) + block, F32),
        vmem((2, 16, 3, 1, 128), F32), vmem((16, 3, 32, 128), F32), vmem((sides,) + block, F32), vmem(block, F32),
        vmem((63, 8, 128), F32), vmem((160, 3072), BF16), vmem((80, 128), F32),
        vmem((32, 128), F32), vmem((32, 128), F32), vmem((share, 128), F32),
        vmem((depth * plane // 2 * share, 128), F32), vmem((share, 128), F32),
        dma((10,)), dma((3, 3)), dma((3, 3)), dma((2,)), dma((2,)), dma((2,)), dma((2,)),
        dma((4,)), dma((4,)), dma((2,)),
        pltpu.SemaphoreType.REGULAR,
    ]
    whole = pl.BlockSpec(memory_space=pltpu.HBM)
    outs = pl.pallas_call(
        functools.partial(kernel, (space, sides, plane, row_count)),
        out_shape=(
            jax.ShapeDtypeStruct((32, 128), F32),
            jax.ShapeDtypeStruct((160, 3072), BF16),
        ),
        in_specs=[whole] * 9 + [pl.BlockSpec(memory_space=smem)],
        out_specs=(whole,) * 2,
        scratch_shapes=scratch,
        compiler_params=pltpu.CompilerParams(
            collective_id=0, has_side_effects=True, vmem_limit_bytes=64 * 1024 * 1024
        ),
    )(
        x_block, basis, material,
        jnp.transpose(k0, (2, 3, 0, 1)), jnp.transpose(ke, (2, 3, 0, 1)),
        diag.T, mass.T, velocities.reshape(8, 128), shifts.reshape(8, 128), sample,
    )
    return pl.pallas_call(
        functools.partial(finish, row_count),
        out_shape=(
            jax.ShapeDtypeStruct(x_block.shape, F32),
            jax.ShapeDtypeStruct((16, 16), F32),
            jax.ShapeDtypeStruct((16, 16), F32),
        ),
        in_specs=[whole] * 2,
        out_specs=(whole,) * 3,
        scratch_shapes=[
            vmem((32, 128), F32), vmem((160, 3072), BF16), vmem((80, 128), F32),
            vmem((32, 256), F32), vmem(block, F32), vmem((16, 16), F32), vmem((16, 16), F32),
            vmem((256, 128), F32), vmem((16, 128), F32), dma((2,)), dma((5,)),
        ],
        compiler_params=pltpu.CompilerParams(vmem_limit_bytes=64 * 1024 * 1024),
    )(*outs)


def solution(mesh):
    in_specs = (
        P(None, None, "space", "basis", None), P("basis", None, "space", None, None),
        P("space", "basis", None), P(), P(), P(), P(), P(), P(), P(),
    )
    out_specs = (P(None, None, "space", "basis", None), P("basis", None), P())
    body = functools.partial(shards, mesh.shape["space"], mesh.shape["basis"])
    return jax.shard_map(body, mesh=mesh, in_specs=in_specs, out_specs=out_specs, check_vma=False)
```

```python
import functools

import jax
import jax.numpy as jnp
from jax import lax
from jax.experimental import pallas as pl
from jax.experimental.pallas import tpu as pltpu
from jax.sharding import PartitionSpec as P

MESH = pl.DeviceIdType.MESH
PLANE = 8
HOLDERS = 4
EXACT = lax.Precision.HIGHEST
F32 = jnp.float32
BF16 = jnp.bfloat16


def dot_exact(a, b):
    return lax.dot_general(
        a, b, (((1,), (0,)), ((), ())), precision=EXACT, preferred_element_type=F32
    )


def iota(shape, axis):
    return lax.broadcasted_iota(jnp.int32, shape, axis)


def pick(bits, values):
    level = list(values)
    for bit in bits:
        level = [jnp.where(bit, level[i + 1], level[i]) for i in range(0, len(level), 2)]
    return level[0]


def fill_fields(mat_ref, k0, ke, diag, mass, velocities, shifts, sample, fields):
    index = sample[0]
    velocity = velocities[index // 128, index % 128]
    shift = shifts[index // 128, index % 128]
    square = velocity * velocity
    cells = mat_ref[0]
    bits = [((cells >> b) & 1) == 1 for b in range(3)]

    def offset_body(o, carry):
        for i in range(3):
            for j in range(3):
                values = [k0[i, j, m, o] - square * ke[i, j, m, o] for m in range(8)]
                fields[o * 9 + i * 3 + j] = pick(bits, values)
        return carry

    lax.fori_loop(0, 7, offset_body, 0)
    for i in range(3):
        values = [diag[i, m] - shift * mass[i, m] for m in range(8)]
        fields[4 * i] = fields[4 * i] + pick(bits, values)


def apply_stencil(xs, xh, yh, fields, applied):
    row = iota((8, 128), 0)
    lane = iota((8, 128), 1)

    def column(n, carry):
        sums = [None] * 3
        for j in range(3):
            centre = xs[n, j]
            low_y = jnp.where(
                row == 0, jnp.broadcast_to(yh[0, n, j], (8, 128)), pltpu.roll(centre, 1, 0)
            )
            high_y = jnp.where(
                row == 7, jnp.broadcast_to(yh[1, n, j], (8, 128)), pltpu.roll(centre, 7, 0)
            )
            low_z = jnp.where(lane == 0, 0.0, pltpu.roll(centre, 1, 1))
            high_z = jnp.where(lane == 127, 0.0, pltpu.roll(centre, 127, 1))
            views = [centre, xh[0, n, j], xh[1, n, j], low_y, high_y, low_z, high_z]
            for o in range(7):
                for i in range(3):
                    term = fields[o * 9 + i * 3 + j] * views[o]
                    sums[i] = term if sums[i] is None else sums[i] + term
        for i in range(3):
            applied[n, i] = sums[i]
        return carry

    lax.fori_loop(0, 16, column, 0)


def split_rows(raw, data, first, part):
    def tile(i, carry):
        t = part * 8 + i
        block = raw[pl.ds(t, 16, stride=24), :]
        high = block.astype(BF16)
        rest = (block - high.astype(F32)).astype(BF16)
        lanes = pl.ds(pl.multiple_of(t * 128, 128), 128)
        data[pl.ds(first, 16), lanes] = high
        data[pl.ds(80 + first, 16), lanes] = rest
        return carry

    lax.fori_loop(0, 8, tile, 0, unroll=True)


def pack_upper(full, packed):
    lane = iota((16, 128), 1)
    rows = [full[16 * g : 16 * g + 16, :] for g in range(5)]
    packed[0:16, :] = jnp.where(lane < 80, rows[0], pltpu.roll(rows[2], 48, 1))
    packed[16:32, :] = jnp.where(
        lane < 64,
        pltpu.roll(rows[1], 112, 1),
        jnp.where(
            lane < 96,
            pltpu.roll(rows[3], 16, 1),
            jnp.where(lane < 112, pltpu.roll(rows[4], 32, 1), 0.0),
        ),
    )


def unpack_full(packed, scale):
    lane = iota((16, 128), 1)
    one, two = packed[0:16, :], packed[16:32, :]
    parts = [
        one,
        pltpu.roll(two, 16, 1),
        pltpu.roll(one, 80, 1),
        pltpu.roll(two, 112, 1),
        pltpu.roll(two, 96, 1),
    ]
    rows = []
    for g in range(5):
        weight = jnp.where(lane < 16 * g + 16, 0.5 * scale, scale)
        rows.append(jnp.where((lane >= 16 * g) & (lane < 80), parts[g] * weight, 0.0))
    rows.append(jnp.zeros((48, 128), F32))
    upper = jnp.concatenate(rows, axis=0)
    return upper + upper.T


def factor(gram, spread, lines):
    lane = iota((8, 128), 1)
    for j in range(16):
        spread[16 * j : 16 * j + 16, :] = jnp.broadcast_to(gram[:, j : j + 1], (16, 128))
    lines[...] = gram

    def full(ref, r):
        return jnp.broadcast_to(ref[r : r + 1, :], (8, 128))

    entry = {(i, j): full(spread, 16 * j + i) for j in range(16) for i in range(j, 16)}
    rows = [
        jnp.where(lane < 16, full(lines, i), jnp.where(lane == 16 + i, 1.0, 0.0))
        for i in range(16)
    ]
    for k in range(16):
        pivot = entry[k, k]
        inverse = 1.0 / pivot
        for i in range(k + 1, 16):
            scale = entry[i, k] * inverse
            for j in range(k + 1, i + 1):
                entry[i, j] = entry[i, j] - scale * entry[j, k]
            rows[i] = rows[i] - scale * rows[k]
        root = lax.rsqrt(pivot)
        root = root * (1.5 - 0.5 * pivot * root * root)
        lines[k : k + 1, :] = (rows[k] * root)[0:1]
    return lines[...]


def kernel(
    sizes,
    x_hbm, basis_hbm, mat_hbm, k0_hbm, ke_hbm, diag_hbm, mass_hbm, vel_hbm, shift_hbm, sample,
    total, data_hbm,
    k0, ke, diag, mass, velocities, shifts,
    mat, xs, xh, yh, whole, raw, applied, fields, data, full, packed, part, zpart, zsum, total_z,
    local_sems, b_send, b_recv, x_send, x_recv, y_send, y_recv, r_send, r_recv, o_sems, ready,
):
    space, sides, plane, row_count = sizes
    depth = space // plane
    lines = plane // 2
    members = sides * 2
    share = 32 // members
    s = lax.axis_index("space")
    b = lax.axis_index("basis")
    z = s // plane
    spot = s - z * plane
    x = spot // 2
    core = spot - 2 * x
    me = b * 2 + core
    place = z * lines + x
    holder = z < HOLDERS
    turn = (depth + HOLDERS) // 2
    served = jnp.where(z < turn, HOLDERS - 1, 0)
    clients = {0: range(turn, depth), HOLDERS - 1: range(HOLDERS, turn)}

    def members_each(act):
        sites = sorted(range(sides), key=lambda d: -min(d, sides - d))
        for dy in sites:
            side = lax.rem(b + dy, sides)
            for other in ((1 - core, core) if dy else (1 - core,)):
                act(side * 2 + other, (z * plane + x * 2 + other, side))

    def spot_at(level, column):
        return level * plane + column * 2 + core, b

    def holders_each(act):
        for level in range(HOLDERS):
            for column in range(lines):
                pl.when(place != level * lines + column)(
                    lambda level=level, column=column: act(spot_at(level, column))
                )

    barrier = pltpu.get_barrier_semaphore()

    def greet(peer):
        pl.semaphore_signal(barrier, inc=1, device_id=peer, device_id_type=MESH)

    beside = s + 2 * core - 1
    has_beside = (beside >= 0) & (beside < space)
    @pl.when(has_beside)
    def _():
        greet((beside, b))

    members_each(lambda index, peer: greet(peer))

    @pl.when(holder)
    def _():
        for level in range(HOLDERS):
            for column in range(lines):
                pl.when(place != level * lines + column)(
                    lambda level=level, column=column: greet(spot_at(level, column))
                )

        @pl.loop(HOLDERS, depth)
        def _(level):
            for column in range(lines):
                greet(spot_at(level, column))

    small = [
        (vel_hbm, velocities), (shift_hbm, shifts), (k0_hbm, k0),
        (ke_hbm, ke), (diag_hbm, diag), (mass_hbm, mass), (mat_hbm, mat),
        (basis_hbm.at[:, :, 0], whole), (x_hbm.at[:, :, 0], xs),
        (basis_hbm.at[:, :, 0, pl.ds(pl.multiple_of(b * 8, 8), 8), :], raw.at[b]),
    ]
    small = [
        pltpu.make_async_copy(source, target, local_sems.at[i])
        for i, (source, target) in enumerate(small)
    ]
    for copy in small:
        copy.start()

    known = members - 1 + HOLDERS * lines
    known = known + jnp.where(has_beside, 1, 0) - jnp.where(holder, 1, 0)
    pl.semaphore_wait(barrier, known)

    @pl.when(jnp.logical_not(holder))
    def _():
        pl.semaphore_signal(
            ready, inc=1, device_id=spot_at(served, x), device_id_type=MESH
        )

    def remote(source, target, send, recv, peer):
        return pltpu.make_async_remote_copy(
            src_ref=source, dst_ref=target, send_sem=send, recv_sem=recv,
            device_id=peer, device_id_type=MESH,
        )

    def basis_copy(k, c):
        side = lax.rem(b + k, sides)
        return remote(
            whole.at[:, c, pl.ds(pl.multiple_of(side * 8, 8), 8), :],
            raw.at[b, :, c], b_send.at[k - 1, c], b_recv.at[k - 1, c], (s, side),
        )

    def x_copy(way):
        peer = s + 1 if way == 0 else s - 1
        return remote(x_hbm.at[:, :, 0], xh.at[way], x_send.at[way], x_recv.at[way], (peer, b))

    def y_copy(way):
        peer = b + 1 if way == 0 else b - 1
        edge = 7 if way == 0 else 0
        return remote(
            x_hbm.at[:, :, 0, edge : edge + 1, :], yh.at[way], y_send.at[way], y_recv.at[way],
            (s, peer),
        )

    x_sends = [s < space - 1, s > 0]
    x_gets = [s > 0, s < space - 1]
    y_sends = [b < sides - 1, b > 0]
    y_gets = [b > 0, b < sides - 1]
    small[7].wait()
    for c in range(3):
        for k in (2, 1, 3):
            basis_copy(k, c).start()
        if c == 1:
            for way in range(2):
                pl.when(y_sends[way])(lambda way=way: y_copy(way).start())
    for way in range(2):
        pl.when(x_sends[way])(lambda way=way: x_copy(way).start())

    for copy in small[:7]:
        copy.wait()
    fill_fields(mat, k0, ke, diag, mass, velocities, shifts, sample, fields)
    small[9].wait()
    own = pl.multiple_of(b * 16, 16)
    for c in range(3):
        split_rows(raw.at[b].reshape(384, 128), data, own, c)
    small[8].wait()

    for way in range(2):
        @pl.when(jnp.logical_not(x_gets[way]))
        def _():
            xh[way] = jnp.zeros(xs.shape, F32)

        @pl.when(jnp.logical_not(y_gets[way]))
        def _():
            yh[way] = jnp.zeros((16, 3, 1, 128), F32)

        pl.when(x_gets[way])(lambda way=way: x_copy(way).wait_recv())
        pl.when(y_gets[way])(lambda way=way: y_copy(way).wait_recv())

    apply_stencil(xs, xh, yh, fields, applied)
    for c in range(3):
        split_rows(applied.reshape(384, 128), data, 64, c)

    products = None
    for c in range(3):
        for k in (1, 3, 2):
            basis_copy(k, c).wait_recv()
            side = lax.rem(b + sides - k, sides)
            split_rows(raw.at[side].reshape(384, 128), data, pl.multiple_of(side * 16, 16), c)
        piece = data[:, c * 1024 : (c + 1) * 1024]
        term = lax.dot_general(
            piece, piece, (((1,), (1,)), ((), ())), preferred_element_type=F32
        )
        products = term if products is None else products + term
    products = products[0:80] + products[80:160]
    full[:, 0:80] = products[:, 0:80] + products[:, 80:160]
    pack_upper(full, packed)

    def rows_of(index):
        return pl.ds(index * share, share)

    def scatter(index, peer):
        remote(
            packed.at[rows_of(index)], part.at[rows_of(me)], r_send.at[0], r_recv.at[0], peer
        ).start()

    def to_holder(peer):
        remote(zpart, zsum.at[rows_of(place)], r_send.at[1], r_recv.at[1], peer).start()

    def to_client(level):
        remote(total_z, total_z, r_send.at[3], r_recv.at[3], spot_at(level, x)).start()

    def gather(index, peer):
        remote(total_z, total.at[rows_of(me)], r_send.at[2], r_recv.at[2], peer).start()

    def fold(ref, count):
        tiles = [ref[8 * i : 8 * i + 8] for i in range(count * share // 8)]
        while len(tiles) > 1:
            half = (len(tiles) + 1) // 2
            tiles = [
                tiles[i] + tiles[i + half] if i + half < len(tiles) else tiles[i]
                for i in range(half)
            ]
        return tiles[0][0:4] + tiles[0][4:8]

    def wait_rows(ref, count, sem):
        view = ref.at[pl.ds(0, count * share)]
        pltpu.make_async_copy(view, view, sem).wait()

    members_each(scatter)
    part[rows_of(me)] = packed[rows_of(me)]
    data_out = pltpu.make_async_copy(data, data_hbm, o_sems.at[0])
    data_out.start()
    wait_rows(part, members - 1, r_recv.at[0])
    zpart[...] = fold(part, members)
    holders_each(to_holder)

    @pl.when(holder)
    def _():
        zsum[rows_of(place)] = zpart[...]
        wait_rows(zsum, depth * lines - 1, r_recv.at[1])
        total_z[...] = fold(zsum, depth * lines)
        members_each(gather)

    for level in clients:
        @pl.when(z == level)
        def _():
            pl.semaphore_wait(ready, len(clients[level]))
            for client in clients[level]:
                to_client(client)

    @pl.when(jnp.logical_not(holder))
    def _():
        wait_rows(total_z, 1, r_recv.at[3])
        members_each(gather)

    own_rows = pltpu.make_async_copy(total_z, total.at[rows_of(me)], o_sems.at[1])
    own_rows.start()
    data_out.wait()
    for c in range(3):
        for k in (1, 2, 3):
            basis_copy(k, c).wait_send()
    for way in range(2):
        pl.when(x_sends[way])(lambda way=way: x_copy(way).wait_send())
        pl.when(y_sends[way])(lambda way=way: y_copy(way).wait_send())
    wait_rows(part, members - 1, r_send.at[0])

    @pl.when(holder)
    def _():
        wait_rows(zsum, HOLDERS * lines - 1, r_send.at[1])

    @pl.when(jnp.logical_not(holder))
    def _():
        wait_rows(zsum, HOLDERS * lines, r_send.at[1])

    for level in clients:
        @pl.when(z == level)
        def _():
            wait_rows(zsum, len(clients[level]), r_send.at[3])

    wait_rows(total, members - 1, r_recv.at[2])
    own_rows.wait()
    wait_rows(total, members - 1, r_send.at[2])


def finish(
    row_count,
    total_hbm, data_hbm, ortho_hbm, coeff_hbm, upper_hbm,
    total, data, full, weights, result, coeff, upper, spread, lines, i_sems, o_sems,
):
    total_in = pltpu.make_async_copy(total_hbm, total, i_sems.at[0])
    total_in.start()
    data_in = pltpu.make_async_copy(data_hbm, data, i_sems.at[1])
    data_in.start()
    own = pl.multiple_of(lax.axis_index("basis") * 16, 16)

    total_in.wait()
    moments = unpack_full(total, 1.0 / row_count)
    lane64 = iota((64, 128), 1)
    first = jnp.where(lane64 < 16, pltpu.roll(moments[0:64], 64, 1), 0.0)
    gram_basis = jnp.where(lane64 < 64, moments[0:64], 0.0)
    zeros64 = jnp.zeros((64, 128), F32)
    both = 2.0 * first - dot_exact(gram_basis, jnp.concatenate([first, zeros64], axis=0))
    full[0:64, :] = both
    coeff[...] = full[pl.ds(own, 16), 0:16]
    coeff_out = pltpu.make_async_copy(coeff, coeff_hbm, o_sems.at[0])
    coeff_out.start()
    unit = jnp.where((iota((64, 128), 0) == lane64) & (lane64 < 16), 1.0, 0.0)
    mix = jnp.concatenate([-both, unit], axis=0)
    image = dot_exact(moments, mix)
    mix_t = mix.T[0:16]
    gram = dot_exact(mix_t, image)
    factors = factor(gram, spread, lines)
    upper[...] = jnp.where(iota((16, 16), 0) <= iota((16, 16), 1), factors[:, 0:16], 0.0)
    upper_out = pltpu.make_async_copy(upper, upper_hbm, o_sems.at[1])
    upper_out.start()
    inverse = pltpu.roll(factors, 112, 1)
    inverse = jnp.where(iota((16, 128), 1) < 16, inverse, 0.0)
    weight = dot_exact(
        inverse, jnp.concatenate([mix_t, jnp.zeros((112, 128), F32)], axis=0)
    )
    high = weight.astype(BF16).astype(F32)
    stacked = jnp.concatenate([high, weight - high], axis=0)
    weights[:, 0:80] = stacked[:, 0:80]
    weights[:, 80:160] = stacked[:, 0:80]
    data_in.wait()
    left = weights[:, 0:160].astype(BF16)
    out = result.reshape(384, 128)
    ortho_out = []
    for c in range(3):
        for t in range(8 * c, 8 * c + 8, 2):
            piece = jnp.dot(
                left, data[:, t * 128 : t * 128 + 256], preferred_element_type=F32
            )
            piece = piece[0:16] + piece[16:32]
            out[pl.ds(t, 16, stride=24), :] = piece[:, 0:128]
            out[pl.ds(t + 1, 16, stride=24), :] = piece[:, 128:256]
        ortho_out.append(
            pltpu.make_async_copy(result.at[:, c], ortho_hbm.at[:, c, 0], o_sems.at[2 + c])
        )
        ortho_out[c].start()
    coeff_out.wait()
    upper_out.wait()
    for copy in ortho_out:
        copy.wait()


def shards(space, sides, x_block, basis, material, k0, diag, ke, mass, velocities, shifts, sample):
    plane = PLANE
    share = 32 // (sides * 2)
    depth = space // plane
    row_count = 3.0 * space * x_block.shape[3] * sides * x_block.shape[4]
    vmem, smem, dma = pltpu.VMEM, pltpu.SMEM, pltpu.SemaphoreType.DMA
    block = (16, 3, 8, 128)
    scratch = [
        smem((3, 3, 8, 7), F32), smem((3, 3, 8, 7), F32), smem((3, 8), F32), smem((3, 8), F32),
        smem((8, 128), F32), smem((8, 128), F32),
        vmem((1, 8, 128), jnp.int32), vmem(block, F32), vmem((2,) + block, F32),
        vmem((2, 16, 3, 1, 128), F32), vmem((16, 3, 32, 128), F32), vmem((sides,) + block, F32), vmem(block, F32),
        vmem((63, 8, 128), F32), vmem((160, 3072), BF16), vmem((80, 128), F32),
        vmem((32, 128), F32), vmem((32, 128), F32), vmem((share, 128), F32),
        vmem((depth * plane // 2 * share, 128), F32), vmem((share, 128), F32),
        dma((10,)), dma((3, 3)), dma((3, 3)), dma((2,)), dma((2,)), dma((2,)), dma((2,)),
        dma((4,)), dma((4,)), dma((2,)),
        pltpu.SemaphoreType.REGULAR,
    ]
    whole = pl.BlockSpec(memory_space=pltpu.HBM)
    outs = pl.pallas_call(
        functools.partial(kernel, (space, sides, plane, row_count)),
        out_shape=(
            jax.ShapeDtypeStruct((32, 128), F32),
            jax.ShapeDtypeStruct((160, 3072), BF16),
        ),
        in_specs=[whole] * 9 + [pl.BlockSpec(memory_space=smem)],
        out_specs=(whole,) * 2,
        scratch_shapes=scratch,
        compiler_params=pltpu.CompilerParams(
            collective_id=0, has_side_effects=True, vmem_limit_bytes=64 * 1024 * 1024
        ),
    )(
        x_block, basis, material,
        jnp.transpose(k0, (2, 3, 0, 1)), jnp.transpose(ke, (2, 3, 0, 1)),
        diag.T, mass.T, velocities.reshape(8, 128), shifts.reshape(8, 128), sample,
    )
    return pl.pallas_call(
        functools.partial(finish, row_count),
        out_shape=(
            jax.ShapeDtypeStruct(x_block.shape, F32),
            jax.ShapeDtypeStruct((16, 16), F32),
            jax.ShapeDtypeStruct((16, 16), F32),
        ),
        in_specs=[whole] * 2,
        out_specs=(whole,) * 3,
        scratch_shapes=[
            vmem((32, 128), F32), vmem((160, 3072), BF16), vmem((80, 128), F32),
            vmem((32, 256), F32), vmem(block, F32), vmem((16, 16), F32), vmem((16, 16), F32),
            vmem((256, 128), F32), vmem((16, 128), F32), dma((2,)), dma((5,)),
        ],
        compiler_params=pltpu.CompilerParams(vmem_limit_bytes=64 * 1024 * 1024),
    )(*outs)


def solution(mesh):
    in_specs = (
        P(None, None, "space", "basis", None), P("basis", None, "space", None, None),
        P("space", "basis", None), P(), P(), P(), P(), P(), P(), P(),
    )
    out_specs = (P(None, None, "space", "basis", None), P("basis", None), P())
    body = functools.partial(shards, mesh.shape["space"], mesh.shape["basis"])
    return jax.shard_map(body, mesh=mesh, in_specs=in_specs, out_specs=out_specs, check_vma=False)
```
